512 devices in a mesh: ctx: 16 (over x, y), clu: 32 (over z, core).
Axes of the slice: x: 4, y: 4, z: 16, core: 2. Of those that a mesh axis runs over, the one named last changes fastest.
Arguments:
- queries: bfloat16 [131072, 1024], P(('ctx', 'clu')), may hold values from -6 to 6
- keys: bfloat16 [131072, 1024], P(('ctx', 'clu')), may hold values from -6 to 6
- values: bfloat16 [131072, 1024], P(('ctx', 'clu')), may hold values from -6 to 6
- clusters: int32 [131072, 8], P(('ctx', 'clu')), may hold values from 0 to 511, as said below
- centroids: float32 [512, 8, 128], P('clu'), may hold values from -0.5 to 0.5
Outputs:
- attended: bfloat16 [131072, 1024], P(('ctx', 'clu'))
- new_centroids: float32 [512, 8, 128], replicated
The draws below stay inside these ranges and needn't reach their ends.
Inputs may be any that keep to these rules, and one draw needn't show every extreme that they name: For each head, the 256 rows of one device name clusters of any one owner (clusters o * 16 to (o + 1) * 16 - 1) at most 32 times, and those of some owner exactly 32 times.
All inputs are finite; a program needn't handle non-finite values.
Results may differ from the reference program's by a relative error of at most 0.018.
Values may be sent and summed in bfloat16 or wider, within the bound.
A program may use at most 64 MiB of HBM per device.

```python
import functools
import math
import jax
import jax.numpy as jnp
from jax import lax

H = 8
DH = 128
C = 512
TOK_DEV = 256
TOKENS = 131072
CAP = 32
N_CTX = 16
N_CLU = 32


def draw_clusters(key, part):
    key = jax.random.fold_in(key, 11)
    n_block = TOKENS // TOK_DEV
    slot_total = N_CLU * CAP
    c_dev = C // N_CLU
    key_hot, key_noise, key_shuffle, key_member = jax.random.split(key, 4)
    hot_owner = jax.random.randint(key_hot, (n_block, H, 1), 0, N_CLU)
    slot_ids = jnp.arange(slot_total, dtype=jnp.int32)
    noise = jax.random.randint(key_noise, (n_block, H, slot_total), 0, 2 ** 16) * slot_total + slot_ids
    slot_score = jnp.where(slot_ids // CAP == hot_owner, slot_ids - slot_total, noise)
    slot_order = jnp.argsort(slot_score, axis=-1)[..., :TOK_DEV]
    shuffle_score = jax.random.randint(key_shuffle, (n_block, H, TOK_DEV), 0, 2 ** 16) * TOK_DEV + jnp.arange(TOK_DEV, dtype=jnp.int32)
    shuffle = jnp.argsort(shuffle_score, axis=-1)
    chosen = jnp.take_along_axis(slot_order, shuffle, axis=-1)
    owners = chosen // CAP
    picked = owners * c_dev + jax.random.randint(key_member, (n_block, H, TOK_DEV), 0, c_dev)
    return jnp.transpose(picked, (0, 2, 1)).reshape(TOKENS, H).astype(jnp.int32)


def level_of(rng, extent, shards, smallest, largest):
    gain = 1.0
    for axis_at, blocks in shards:
        draws = jax.random.uniform(jax.random.fold_in(jax.random.fold_in(rng, 6), axis_at), (blocks,), jnp.float32, smallest / len(shards), largest / len(shards))
        gain = gain * jnp.repeat(jnp.exp(draws), extent[axis_at] // blocks).reshape((-1,) + (1,) * (len(extent) - 1 - axis_at))
    return gain


def normal_values(own_key, shape, deviation, bound, pieces=(), held_as=jnp.bfloat16):
    result = jax.random.normal(own_key, shape, jnp.float32) * deviation
    if len(pieces) > 0:
        result = level_of(own_key, shape, pieces, -0.22, 0.18) * result
    return jnp.clip(result, min=-bound, max=bound).astype(held_as)


def setup_inputs(seed: int = 0) -> dict:
    streams_of = jax.random.split(jax.random.key(seed), 6)
    queries = normal_values(streams_of[0], (TOKENS, H * DH), 1.0, 6.0, ((0, 512),))
    keys = normal_values(streams_of[1], (TOKENS, H * DH), 1.0, 6.0, ((0, 512),))
    values = normal_values(streams_of[2], (TOKENS, H * DH), 1.0, 6.0, ((0, 512),))
    clusters = draw_clusters(jax.random.fold_in(streams_of[5], 71), 0)
    centroids = normal_values(streams_of[4], (C, H, DH), DH ** -0.5, 0.5, ((0, 32),), jnp.float32)
    return {"queries": queries, "keys": keys, "values": values, "clusters": clusters, "centroids": centroids}


EPS = 1e-06
SCALE = 8.0
DECAY = 0.75

def unit_rows(rows):
    floats = rows.astype(jnp.float32)
    factor = lax.rsqrt(lax.optimization_barrier(jnp.mean(floats * floats, axis=-1, keepdims=True)) + EPS) / math.sqrt(floats.shape[-1])
    return (floats * factor).astype(jnp.bfloat16)

def pack_rows(queries, keys, values, clusters, n_owner, cap, c_dev):
    tok_count, head_count = clusters.shape
    head_size = queries.shape[1] // head_count
    query_rows = unit_rows(queries.reshape(tok_count, head_count, head_size))
    key_rows = unit_rows(keys.reshape(tok_count, head_count, head_size))
    value_rows = values.reshape(tok_count, head_count, head_size)
    owners = clusters // c_dev
    member = clusters % c_dev
    onehot = (owners[:, :, None] == jnp.arange(n_owner, dtype=jnp.int32)[None, None, :]).astype(jnp.int32)
    slot_rank = lax.optimization_barrier(jnp.sum((jnp.cumsum(onehot, axis=0) - onehot) * onehot, axis=-1)).astype(jnp.int32)
    head_idx = jnp.broadcast_to(jnp.arange(head_count, dtype=jnp.int32)[None, :], (tok_count, head_count))
    tok_idx = jnp.broadcast_to(jnp.arange(tok_count, dtype=jnp.int32)[:, None], (tok_count, head_count))

    def place(rows):
        return jnp.zeros((n_owner, head_count, cap, head_size), jnp.bfloat16).at[owners, head_idx, slot_rank].set(rows)
    codes = jnp.zeros((n_owner, head_count, cap), jnp.int32).at[owners, head_idx, slot_rank].set(tok_idx * (c_dev + 1) + member + 1)
    return ((place(query_rows), place(key_rows), place(value_rows), codes), owners, head_idx, slot_rank)

def attend_one(query_slots, key_slots, value_slots, meta_slots, tok_dev, c_dev):
    n_source, cap, head_size = query_slots.shape
    total_rows = n_source * cap
    query_rows = query_slots.reshape(total_rows, head_size)
    key_rows = key_slots.reshape(total_rows, head_size)
    value_rows = value_slots.reshape(total_rows, head_size)
    codes = meta_slots.reshape(total_rows)
    member = codes % (c_dev + 1)
    position = jnp.arange(total_rows, dtype=jnp.int32) // cap * tok_dev + codes // (c_dev + 1)
    scores = jnp.dot(query_rows, key_rows.T, preferred_element_type=jnp.float32) * SCALE
    allowed = (member[:, None] == member[None, :]) & (position[None, :] <= position[:, None])
    weights = jnp.where(allowed, jnp.exp(scores), jnp.float32(0.0))
    probs = (weights / lax.optimization_barrier(jnp.sum(weights, axis=-1, keepdims=True))).astype(jnp.bfloat16)
    mixed = jnp.dot(probs, value_rows, preferred_element_type=jnp.float32).astype(jnp.bfloat16)
    selector = (member[None, :] == jnp.arange(1, c_dev + 1, dtype=jnp.int32)[:, None]).astype(jnp.bfloat16)
    sums = jnp.dot(selector, query_rows, preferred_element_type=jnp.float32) + jnp.dot(selector, key_rows, preferred_element_type=jnp.float32)
    return (mixed.reshape(n_source, cap, head_size), sums)

def attend_heads(query_slots, key_slots, value_slots, meta_slots, tok_dev, c_dev):

    def per_head(items):
        return attend_one(items[0], items[1], items[2], items[3], tok_dev, c_dev)
    mixed, sums = lax.map(per_head, (jnp.moveaxis(query_slots, 1, 0), jnp.moveaxis(key_slots, 1, 0), jnp.moveaxis(value_slots, 1, 0), jnp.moveaxis(meta_slots, 1, 0)))
    return (jnp.moveaxis(mixed, 0, 1), jnp.moveaxis(sums, 0, 1))

def reference(queries, keys, values, clusters, centroids):
    n_owner = N_CLU
    c_dev = C // N_CLU
    width = H * DH
    packer = functools.partial(pack_rows, n_owner=n_owner, cap=CAP, c_dev=c_dev)

    def one_group(items):
        group_q, group_k, group_v, group_c = items
        packed, owners, head_idx, slot_rank = jax.vmap(packer)(group_q, group_k, group_v, group_c)
        arrived = tuple((jnp.swapaxes(piece, 0, 1) for piece in packed))

        def per_owner(parts):
            return attend_heads(parts[0], parts[1], parts[2], parts[3], TOK_DEV, c_dev)
        mixed, sums = lax.map(per_owner, arrived)
        back = jnp.swapaxes(mixed, 0, 1)

        def pick(returned, owner_ids, head_ids, rank_ids):
            return returned[owner_ids, head_ids, rank_ids].reshape(TOK_DEV, width)
        return (jax.vmap(pick)(back, owners, head_idx, slot_rank), sums)
    shaped = (queries.reshape(N_CTX, N_CLU, TOK_DEV, width), keys.reshape(N_CTX, N_CLU, TOK_DEV, width), values.reshape(N_CTX, N_CLU, TOK_DEV, width), clusters.reshape(N_CTX, N_CLU, TOK_DEV, H))
    outputs, sums = lax.map(one_group, shaped)
    total = lax.optimization_barrier(jnp.sum(sums, axis=0)).reshape(C, H, DH)
    fresh = DECAY * centroids + (1.0 - DECAY) / 2.0 * total
    return (outputs.reshape(TOKENS, width), fresh)
```

```python
import functools
import math

import jax
import jax.numpy as jnp
from jax import lax
from jax.experimental import pallas as pl
from jax.experimental.pallas import tpu as pltpu
from jax.sharding import PartitionSpec as P

MESH = pl.DeviceIdType.MESH
EPS = 1e-06
SCALE = 8.0
DECAY = 0.75
D = 128
GAP = 64.0

BF = jnp.bfloat16
F32 = jnp.float32


def unit(rows):
    factor = lax.rsqrt(jnp.mean(rows * rows, axis=-1, keepdims=True) + EPS) / math.sqrt(D)
    return (rows * factor).astype(BF)


def kernel(
    n_ctx,
    n_clu,
    q_ref,
    k_ref,
    v_ref,
    clt_ref,
    cent_ref,
    out_ref,
    newc_ref,
    kst,
    nrm,
    kbuf,
    vbuf,
    qbuf,
    obuf,
    acc,
    sst,
    sin,
    zst,
    zin,
    fin,
    vs,
    vr,
    ks,
    kr,
    qs,
    qr,
    vfs,
    vfr,
    kfs,
    kfr,
    os_,
    or_,
    xs,
    xr,
    zs,
    zr,
    fs,
    fr,
    gs,
    gr,
):
    tok = q_ref.shape[0]
    heads = q_ref.shape[1] // D
    n_z = n_clu // 2
    step = n_z // heads
    bits = max(1, (n_ctx * n_clu - 1).bit_length())

    col = lax.axis_index("ctx")
    me = lax.axis_index("clu")
    z = me // 2
    core = lax.rem(me, 2)
    sib = (col, me + 1 - 2 * core)
    is_home = lax.rem(z, step) == 0
    my_head = z // step

    def spread(i, base, n):
        off = jnp.where(lax.rem(i, 2) == 1, (i + 1) // 2, n - i // 2)
        return lax.rem(base + off, n)

    def remote(src, dst, send, recv, dev):
        return pltpu.make_async_remote_copy(
            src_ref=src, dst_ref=dst, send_sem=send, recv_sem=recv, device_id=dev, device_id_type=MESH
        )

    def lanes(h):
        return pl.ds(pl.multiple_of(h * D, D), D)

    barrier = pltpu.get_barrier_semaphore()

    def greet_clu(i, c):
        pl.semaphore_signal(barrier, inc=1, device_id=(col, lax.rem(me + i, n_clu)), device_id_type=MESH)
        return c

    def greet_ctx(i, c):
        pl.semaphore_signal(barrier, inc=1, device_id=(lax.rem(col + i, n_ctx), me), device_id_type=MESH)
        return c

    lax.fori_loop(1, n_clu, greet_clu, 0)
    lax.fori_loop(1, n_ctx, greet_ctx, 0)
    pl.semaphore_wait(barrier, n_clu - 1 + n_ctx - 1)

    def v_src(h):
        return v_ref.at[:, lanes(h)]

    def q_src(h):
        return nrm.at[h, :, pl.ds(0, D)]

    def v_dst(c):
        return vbuf.at[c, :, pl.ds(0, D)]

    def k_dst(c):
        return kbuf.at[c, pl.ds(0, D + 16), :]

    def to_home(h, src, dst, send, recv):
        target = h * step

        @pl.when(target == z)
        def _():
            pltpu.make_async_copy(src, dst, recv.at[z]).start()

        @pl.when(target != z)
        def _():
            remote(src, dst, send.at[h], recv.at[z], (col, target * 2 + core)).start()

    def sent_home(h, src, dst, send, recv):
        target = h * step

        @pl.when(target != z)
        def _():
            remote(src, dst, send.at[h], recv.at[z], (col, target * 2 + core)).wait_send()

    def send_v(i, c):
        h = spread(i, z // step, heads)
        to_home(h, v_src(h), v_dst(me), vs, vr)
        return c

    lax.fori_loop(0, heads, send_v, 0)

    row_id = lax.broadcasted_iota(jnp.int32, (16, tok), 0)

    def send_k(i, c):
        h = spread(i, z // step, heads)
        kn = unit(k_ref[:, lanes(h)].astype(F32))
        qn = unit(q_ref[:, lanes(h)].astype(F32))
        nrm[h, :, pl.ds(0, D)] = qn
        nrm[h, :, pl.ds(D, D)] = kn
        kst[h, pl.ds(0, D), :] = jnp.transpose(kn.astype(F32)).astype(BF)
        ids = clt_ref[pl.ds(h, 1), :]
        code = 2 * (lax.shift_right_logical(jnp.broadcast_to(ids, (16, tok)), row_id) & 1) - 1
        code = jnp.where(row_id < bits, code, jnp.where(row_id == bits, 1, 0))
        kst[h, pl.ds(D, 16), :] = code.astype(F32).astype(BF)
        to_home(h, kst.at[h], k_dst(me), ks, kr)
        return c

    lax.fori_loop(0, heads, send_k, 0)

    def send_q(i, c):
        h = spread(i, z // step, heads)
        to_home(h, q_src(h), qbuf.at[z], qs, qr)
        return c

    lax.fori_loop(0, heads, send_q, 0)

    n_row = n_ctx * n_clu
    sum_row = lax.broadcasted_iota(jnp.int32, (n_row, tok), 0)

    def sum_head(h, c):
        ids = clt_ref[pl.ds(h, 1), :]
        place = lax.rem(ids, n_ctx) * n_clu + ids // n_ctx
        pick = jnp.where(sum_row == place, 1.0, 0.0).astype(BF)
        both = jnp.dot(pick, nrm[h], preferred_element_type=F32)
        both = both[:, :D] + both[:, D:]
        sst[:, h, :, :] = both.reshape(n_ctx, n_clu, D).astype(BF)
        return c

    lax.fori_loop(0, heads, sum_head, 0)

    def x_copy(c):
        return remote(sst.at[c], sin.at[col], xs.at[c], xr.at[col], (c, me))

    def x_start(i, c):
        x_copy(lax.rem(col + i, n_ctx)).start()
        return c

    lax.fori_loop(1, n_ctx, x_start, 0)
    sin[col] = sst[col]

    @pl.when(is_home)
    def _():
        def fill(c, carry):
            vbuf[c, :, pl.ds(D, D)] = jnp.ones((tok, D), BF)
            kbuf[c, pl.ds(D + 16, D - 16), :] = jnp.zeros((D - 16, tok), BF)
            return carry

        lax.fori_loop(0, n_clu, fill, 0)

    def x_wait(i, c):
        other = lax.rem(col + i, n_ctx)
        pltpu.make_async_copy(sin.at[other], sin.at[other], xr.at[other]).wait()
        return c

    lax.fori_loop(1, n_ctx, x_wait, 0)
    for h in range(heads):
        part = sin[0, h].astype(F32)
        for c in range(1, n_ctx):
            part = part + sin[c, h].astype(F32)
        zst[pl.ds(h, n_clu, stride=heads), :] = part

    def z_src(o):
        return zst.at[pl.ds(pl.multiple_of(o * heads, heads), heads), :]

    def z_copy(o):
        return remote(z_src(o), zin.at[me], zs.at[o], zr.at[me], (col, o))

    def z_start(i, c):
        z_copy(lax.rem(me + i, n_clu)).start()
        return c

    lax.fori_loop(1, n_clu, z_start, 0)
    zin[me] = zst[pl.ds(pl.multiple_of(me * heads, heads), heads), :]

    def z_wait(i, c):
        o = lax.rem(me + i, n_clu)
        pltpu.make_async_copy(zin.at[o], zin.at[o], zr.at[o]).wait()
        return c

    lax.fori_loop(1, n_clu, z_wait, 0)
    total = jnp.sum(zin[...], axis=0)
    fin[me] = DECAY * cent_ref[col] + (1.0 - DECAY) / 2.0 * total

    def f_copy(o):
        return remote(fin.at[me], fin.at[me], fs.at[o], fr.at[me], (col, o))

    def f_start(i, c):
        f_copy(lax.rem(me + i, n_clu)).start()
        return c

    lax.fori_loop(1, n_clu, f_start, 0)

    def f_wait(i, c):
        o = lax.rem(me + i, n_clu)
        pltpu.make_async_copy(fin.at[o], fin.at[o], fr.at[o]).wait()
        return c

    lax.fori_loop(1, n_clu, f_wait, 0)

    def g_copy(c):
        return remote(fin, newc_ref.at[:, col], gs.at[c], gr.at[col], (c, me))

    def g_start(i, c):
        g_copy(lax.rem(col + i, n_ctx)).start()
        return c

    lax.fori_loop(1, n_ctx, g_start, 0)
    own_fresh = pltpu.make_async_copy(fin, newc_ref.at[:, col], gr.at[col])
    own_fresh.start()

    def v_pass(t):
        c = 2 * t + core
        return remote(v_dst(c), v_dst(c), vfs.at[t], vfr.at[t], sib)

    def k_pass(t):
        c = 2 * t + core
        return remote(k_dst(c), k_dst(c), kfs.at[t], kfr.at[t], sib)

    def out_dst(h):
        return out_ref.at[:, lanes(h)]

    def o_copy(t):
        return remote(obuf.at[t], out_dst(my_head), os_.at[t], or_.at[my_head], (col, 2 * t + core))

    def own_copy():
        return pltpu.make_async_copy(obuf.at[z], out_dst(my_head), or_.at[my_head])

    @pl.when(is_home)
    def _():
        def pass_v(i, c):
            t = spread(i, z, n_z)
            pltpu.make_async_copy(v_dst(2 * t + core), v_dst(2 * t + core), vr.at[t]).wait()
            v_pass(t).start()
            return c

        lax.fori_loop(0, n_z, pass_v, 0)

        def pass_k(i, c):
            t = spread(i, z, n_z)
            pltpu.make_async_copy(k_dst(2 * t + core), k_dst(2 * t + core), kr.at[t]).wait()
            k_pass(t).start()
            return c

        lax.fori_loop(0, n_z, pass_k, 0)

        def arrive(i, c):
            t = spread(i, z, n_z)
            o = 2 * t + 1 - core
            pltpu.make_async_copy(v_dst(o), v_dst(o), vfr.at[t]).wait()
            pltpu.make_async_copy(k_dst(o), k_dst(o), kfr.at[t]).wait()
            return c

        lax.fori_loop(0, n_z, arrive, 0)

        lane = lax.broadcasted_iota(jnp.int32, (tok, D), 1)
        weight = jnp.where(lane < bits, GAP, jnp.where(lane == bits, -GAP * bits, 0.0))
        key_at = lax.broadcasted_iota(jnp.int32, (tok, tok), 1)
        query_at = lax.broadcasted_iota(jnp.int32, (tok, tok), 0) + core * tok

        def attend(i, carry):
            t = spread(i, z, n_z)
            pltpu.make_async_copy(qbuf.at[t], qbuf.at[t], qr.at[t]).wait()
            mine = qbuf[t].astype(F32) * SCALE
            code = jnp.transpose(kbuf[2 * t + core, pl.ds(D, D), :].astype(F32)) * weight
            query = jnp.concatenate([mine, code], axis=1).astype(BF)

            def scores(c):
                return jnp.exp(jnp.dot(query, kbuf[c], preferred_element_type=F32))

            def mix(p, c):
                return jnp.dot(p.astype(BF), vbuf[c], preferred_element_type=F32)

            p0 = jnp.where(key_at <= query_at, scores(2 * t), 0.0)
            p1 = jnp.where(key_at + tok <= query_at, scores(2 * t + 1), 0.0)
            acc[...] = mix(p0, 2 * t) + mix(p1, 2 * t + 1)

            def earlier(u, c):
                acc[...] += mix(scores(2 * u), 2 * u) + mix(scores(2 * u + 1), 2 * u + 1)
                return c

            lax.fori_loop(0, t, earlier, 0)
            obuf[t] = (acc[:, pl.ds(0, D)] / acc[:, pl.ds(D, D)]).astype(BF)

            @pl.when(t == z)
            def _():
                own_copy().start()

            @pl.when(t != z)
            def _():
                o_copy(t).start()

            return carry

        lax.fori_loop(0, n_z, attend, 0)

        def done(i, c):
            t = lax.rem(z + i, n_z)
            v_pass(t).wait_send()
            k_pass(t).wait_send()

            @pl.when(t != z)
            def _():
                o_copy(t).wait_send()

            return c

        lax.fori_loop(0, n_z, done, 0)

    def o_wait(h, c):
        pltpu.make_async_copy(out_dst(h), out_dst(h), or_.at[h]).wait()
        return c

    lax.fori_loop(0, heads, o_wait, 0)

    def g_wait(c, carry):
        pltpu.make_async_copy(newc_ref.at[:, c], newc_ref.at[:, c], gr.at[c]).wait()
        return carry

    lax.fori_loop(0, n_ctx, g_wait, 0)

    def home_sent(h, c):
        sent_home(h, v_src(h), v_dst(me), vs, vr)
        sent_home(h, kst.at[h], k_dst(me), ks, kr)
        sent_home(h, q_src(h), qbuf.at[z], qs, qr)
        return c

    lax.fori_loop(0, heads, home_sent, 0)

    def ctx_sent(i, c):
        other = lax.rem(col + i, n_ctx)
        x_copy(other).wait_send()
        g_copy(other).wait_send()
        return c

    lax.fori_loop(1, n_ctx, ctx_sent, 0)

    def clu_sent(i, c):
        o = lax.rem(me + i, n_clu)
        z_copy(o).wait_send()
        f_copy(o).wait_send()
        return c

    lax.fori_loop(1, n_clu, clu_sent, 0)


def local(n_ctx, n_clu, queries, keys, values, clusters, centroids):
    tok, width = queries.shape
    heads = width // D
    n_z = n_clu // 2
    vmem = pl.BlockSpec(memory_space=pltpu.VMEM)
    hbm = pl.BlockSpec(memory_space=pl.ANY)
    dma = pltpu.SemaphoreType.DMA
    attended, fresh = pl.pallas_call(
        functools.partial(kernel, n_ctx, n_clu),
        out_shape=(
            jax.ShapeDtypeStruct((tok, width), BF),
            jax.ShapeDtypeStruct((n_clu, n_ctx, heads, D), F32),
        ),
        in_specs=[vmem] * 5,
        out_specs=(hbm, hbm),
        scratch_shapes=[
            pltpu.VMEM((heads, D + 16, tok), BF),
            pltpu.VMEM((heads, tok, 2 * D), BF),
            pltpu.VMEM((n_clu, 2 * D, tok), BF),
            pltpu.VMEM((n_clu, tok, 2 * D), BF),
            pltpu.VMEM((n_z, tok, D), BF),
            pltpu.VMEM((n_z, tok, D), BF),
            pltpu.VMEM((tok, 2 * D), F32),
            pltpu.VMEM((n_ctx, heads, n_clu, D), BF),
            pltpu.VMEM((n_ctx, heads, n_clu, D), BF),
            pltpu.VMEM((n_clu * heads, D), F32),
            pltpu.VMEM((n_clu, heads, D), F32),
            pltpu.VMEM((n_clu, heads, D), F32),
            dma((heads,)),
            dma((n_z,)),
            dma((heads,)),
            dma((n_z,)),
            dma((heads,)),
            dma((n_z,)),
            dma((n_z,)),
            dma((n_z,)),
            dma((n_z,)),
            dma((n_z,)),
            dma((n_z,)),
            dma((heads,)),
            dma((n_ctx,)),
            dma((n_ctx,)),
            dma((n_clu,)),
            dma((n_clu,)),
            dma((n_clu,)),
            dma((n_clu,)),
            dma((n_ctx,)),
            dma((n_ctx,)),
        ],
        compiler_params=pltpu.CompilerParams(
            collective_id=0, has_side_effects=True, vmem_limit_bytes=40 * 1024 * 1024
        ),
        cost_estimate=pl.CostEstimate(
            flops=2 * 2 * 2 * D * tok * tok * n_clu * n_clu // 4,
            bytes_accessed=8 * tok * width,
            transcendentals=tok * tok * n_clu * n_clu // 4,
        ),
    )(queries, keys, values, clusters.T, centroids)
    return attended, fresh.reshape(n_clu * n_ctx, heads, D)


def solution(mesh):
    placed = (
        P(("ctx", "clu"), None),
        P(("ctx", "clu"), None),
        P(("ctx", "clu"), None),
        P(("ctx", "clu"), None),
        P("clu", None, None),
    )
    return jax.shard_map(
        functools.partial(local, mesh.shape["ctx"], mesh.shape["clu"]),
        mesh=mesh,
        in_specs=placed,
        out_specs=(P(("ctx", "clu"), None), P()),
        check_vma=False,
    )
```

```python
import functools
import math

import jax
import jax.numpy as jnp
from jax import lax
from jax.experimental import pallas as pl
from jax.experimental.pallas import tpu as pltpu
from jax.sharding import PartitionSpec as P

MESH = pl.DeviceIdType.MESH
EPS = 1e-06
SCALE = 8.0
DECAY = 0.75
D = 128
GAP = 64.0

BF = jnp.bfloat16
F32 = jnp.float32


def unit(rows):
    factor = lax.rsqrt(jnp.mean(rows * rows, axis=-1, keepdims=True) + EPS) / math.sqrt(D)
    return (rows * factor).astype(BF)


def kernel(
    n_ctx,
    n_clu,
    q_ref,
    k_ref,
    v_ref,
    clt_ref,
    cent_ref,
    out_ref,
    newc_ref,
    qin,
    kin,
    ids,
    cen,
    kst,
    nrm,
    kbuf,
    vbuf,
    qbuf,
    obuf,
    acc,
    sst,
    sin,
    zst,
    zin,
    fin,
    fnb,
    ls,
    vs,
    vr,
    ks,
    kr,
    qs,
    qr,
    vfs,
    vfr,
    kfs,
    kfr,
    os_,
    or_,
    xs,
    xr,
    zs,
    zr,
    fs,
    fr,
    gs,
    gr,
):
    tok = q_ref.shape[0]
    heads = q_ref.shape[1] // D
    n_z = n_clu // 2
    step = n_z // heads
    bits = max(1, (n_ctx * n_clu - 1).bit_length())

    col = lax.axis_index("ctx")
    me = lax.axis_index("clu")
    z = me // 2
    core = lax.rem(me, 2)
    sib = (col, me + 1 - 2 * core)
    is_home = lax.rem(z, step) == 0
    my_head = z // step

    def spread(i, base, n):
        j = n - 1 - i
        off = jnp.where(lax.rem(j, 2) == 1, (j + 1) // 2, n - j // 2)
        return lax.rem(base + off, n)

    def remote(src, dst, send, recv, dev):
        return pltpu.make_async_remote_copy(
            src_ref=src, dst_ref=dst, send_sem=send, recv_sem=recv, device_id=dev, device_id_type=MESH
        )

    def lanes(h):
        return pl.ds(pl.multiple_of(h * D, D), D)

    barrier = pltpu.get_barrier_semaphore()

    def greet_clu(i, c):
        pl.semaphore_signal(barrier, inc=1, device_id=(col, lax.rem(me + i, n_clu)), device_id_type=MESH)
        return c

    def greet_ctx(i, c):
        pl.semaphore_signal(barrier, inc=1, device_id=(lax.rem(col + i, n_ctx), me), device_id_type=MESH)
        return c

    loads = [
        pltpu.make_async_copy(src, dst, ls.at[i])
        for i, (src, dst) in enumerate(((k_ref, kin), (q_ref, qin), (clt_ref, ids), (cent_ref, cen)))
    ]
    for load in loads:
        load.start()
    lax.fori_loop(1, n_clu, greet_clu, 0)
    lax.fori_loop(1, n_ctx, greet_ctx, 0)
    pl.semaphore_wait(barrier, n_clu - 1 + n_ctx - 1)

    def v_src(h):
        return v_ref.at[:, lanes(h)]

    def q_src(h):
        return nrm.at[h, :, pl.ds(0, D)]

    def v_dst(c):
        return vbuf.at[c, :, pl.ds(0, D)]

    def k_dst(c):
        return kbuf.at[c, pl.ds(0, D + 16), :]

    def to_home(h, src, dst, send, recv):
        target = h * step

        @pl.when(target == z)
        def _():
            pltpu.make_async_copy(src, dst, recv.at[z]).start()

        @pl.when(target != z)
        def _():
            remote(src, dst, send.at[h], recv.at[z], (col, target * 2 + core)).start()

    def sent_home(h, src, dst, send, recv):
        target = h * step

        @pl.when(target != z)
        def _():
            remote(src, dst, send.at[h], recv.at[z], (col, target * 2 + core)).wait_send()

    def send_v(i, c):
        h = spread(i, z // step, heads)
        to_home(h, v_src(h), v_dst(me), vs, vr)
        return c

    lax.fori_loop(0, heads, send_v, 0)

    for load in loads:
        load.wait()

    row_id = lax.broadcasted_iota(jnp.int32, (16, tok), 0)

    def ready_head(i, c):
        h = spread(i, z // step, heads)
        kn = unit(kin[:, lanes(h)].astype(F32))
        qn = unit(qin[:, lanes(h)].astype(F32))
        nrm[h, :, pl.ds(0, D)] = qn
        nrm[h, :, pl.ds(D, D)] = kn
        kst[h, pl.ds(0, D), :] = jnp.transpose(kn.astype(F32)).astype(BF)
        row = jnp.broadcast_to(ids[pl.ds(h, 1), :], (16, tok))
        code = 2 * (lax.shift_right_logical(row, row_id) & 1) - 1
        code = jnp.where(row_id < bits, code, jnp.where(row_id == bits, 1, 0))
        kst[h, pl.ds(D, 16), :] = code.astype(F32).astype(BF)
        return c

    lax.fori_loop(0, heads, ready_head, 0)

    def send_k(i, c):
        h = spread(i, z // step, heads)
        to_home(h, kst.at[h], k_dst(me), ks, kr)
        return c

    def send_q(i, c):
        h = spread(i, z // step, heads)
        to_home(h, q_src(h), qbuf.at[z], qs, qr)
        return c

    lax.fori_loop(0, heads // 2, send_k, 0)

    n_row = n_ctx * n_clu
    sum_row = lax.broadcasted_iota(jnp.int32, (n_row, tok), 0)

    def sum_head(h, c):
        row = ids[pl.ds(h, 1), :]
        place = lax.rem(row, n_ctx) * n_clu + row // n_ctx
        pick = jnp.where(sum_row == place, 1.0, 0.0).astype(BF)
        both = jnp.dot(pick, nrm[h], preferred_element_type=F32)
        both = both[:, :D] + both[:, D:]
        sst[:, h, :, :] = both.reshape(n_ctx, n_clu, D).astype(BF)
        return c

    lax.fori_loop(0, heads, sum_head, 0)

    def x_copy(c):
        return remote(sst.at[c], sin.at[col], xs.at[c], xr.at[col], (c, me))

    def x_start(i, c):
        x_copy(lax.rem(col + i, n_ctx)).start()
        return c

    lax.fori_loop(1, n_ctx, x_start, 0)
    sin[col] = sst[col]

    @pl.when(is_home)
    def _():
        def fill(c, carry):
            vbuf[c, :, pl.ds(D, D)] = jnp.ones((tok, D), BF)
            kbuf[c, pl.ds(D + 16, D - 16), :] = jnp.zeros((D - 16, tok), BF)
            return carry

        lax.fori_loop(0, n_clu, fill, 0)

    def x_wait(i, c):
        other = lax.rem(col + i, n_ctx)
        pltpu.make_async_copy(sin.at[other], sin.at[other], xr.at[other]).wait()
        return c

    lax.fori_loop(1, n_ctx, x_wait, 0)
    for h in range(heads):
        part = sin[0, h].astype(F32)
        for c in range(1, n_ctx):
            part = part + sin[c, h].astype(F32)
        zst[pl.ds(h, n_clu, stride=heads), :] = part

    def z_src(o):
        return zst.at[pl.ds(pl.multiple_of(o * heads, heads), heads), :]

    def z_copy(o):
        return remote(z_src(o), zin.at[me], zs.at[o], zr.at[me], (col, o))

    def z_start(i, c):
        z_copy(lax.rem(me + i, n_clu)).start()
        return c

    lax.fori_loop(1, n_clu, z_start, 0)
    lax.fori_loop(heads // 2, heads, send_k, 0)
    zin[me] = zst[pl.ds(pl.multiple_of(me * heads, heads), heads), :]

    def v_pass(t):
        c = 2 * t + core
        return remote(v_dst(c), v_dst(c), vfs.at[t], vfr.at[t], sib)

    def k_pass(t):
        c = 2 * t + core
        return remote(k_dst(c), k_dst(c), kfs.at[t], kfr.at[t], sib)

    @pl.when(is_home)
    def _():
        def pass_v(i, c):
            t = spread(i, z, n_z)
            pltpu.make_async_copy(v_dst(2 * t + core), v_dst(2 * t + core), vr.at[t]).wait()
            v_pass(t).start()
            return c

        lax.fori_loop(0, n_z, pass_v, 0)

    def z_wait(i, c):
        o = lax.rem(me + i, n_clu)
        pltpu.make_async_copy(zin.at[o], zin.at[o], zr.at[o]).wait()
        return c

    lax.fori_loop(1, n_clu, z_wait, 0)
    total = jnp.sum(zin[...], axis=0)
    fin[me] = DECAY * cen[col] + (1.0 - DECAY) / 2.0 * total

    def f_copy(o):
        return remote(fin.at[me], fin.at[me], fs.at[o], fr.at[me], (col, o))

    def f_start(i, c):
        f_copy(lax.rem(me + i, n_clu)).start()
        return c

    lax.fori_loop(1, n_clu, f_start, 0)
    lax.fori_loop(0, heads, send_q, 0)

    @pl.when(is_home)
    def _():
        def pass_k(i, c):
            t = spread(i, z, n_z)
            pltpu.make_async_copy(k_dst(2 * t + core), k_dst(2 * t + core), kr.at[t]).wait()
            k_pass(t).start()
            return c

        lax.fori_loop(0, n_z, pass_k, 0)

    def f_wait(i, c):
        o = lax.rem(me + i, n_clu)
        pltpu.make_async_copy(fin.at[o], fin.at[o], fr.at[o]).wait()
        return c

    lax.fori_loop(1, n_clu, f_wait, 0)
    fnb[...] = fin[...].reshape(n_clu * heads, D).astype(BF)

    def g_copy(c):
        return remote(fnb, newc_ref.at[col], gs.at[c], gr.at[col], (c, me))

    def g_start(i, c):
        g_copy(lax.rem(col + i, n_ctx)).start()
        return c

    lax.fori_loop(1, n_ctx, g_start, 0)
    own_fresh = pltpu.make_async_copy(fnb, newc_ref.at[col], gr.at[col])
    own_fresh.start()

    def out_dst(h):
        return out_ref.at[:, lanes(h)]

    def o_copy(t):
        return remote(obuf.at[t], out_dst(my_head), os_.at[t], or_.at[my_head], (col, 2 * t + core))

    def own_copy():
        return pltpu.make_async_copy(obuf.at[z], out_dst(my_head), or_.at[my_head])

    @pl.when(is_home)
    def _():
        def arrive(i, c):
            t = spread(i, z, n_z)
            o = 2 * t + 1 - core
            pltpu.make_async_copy(v_dst(o), v_dst(o), vfr.at[t]).wait()
            pltpu.make_async_copy(k_dst(o), k_dst(o), kfr.at[t]).wait()
            return c

        lax.fori_loop(0, n_z, arrive, 0)

        n_q, n_k = 2, 4
        lane = lax.broadcasted_iota(jnp.int32, (n_q * tok, D), 1)
        weight = jnp.where(lane < bits, GAP, jnp.where(lane == bits, -GAP * bits, 0.0))
        key_at = lax.broadcasted_iota(jnp.int32, (n_q * tok, tok), 1)
        row_at = lax.broadcasted_iota(jnp.int32, (n_q * tok, tok), 0)
        query_at = (2 * (row_at // tok) + core) * tok + lax.rem(row_at, tok)

        def attend(i, carry):
            s = spread(i, z // n_q, n_z // n_q)
            codes = []
            for j in range(n_q):
                t = n_q * s + j
                pltpu.make_async_copy(qbuf.at[t], qbuf.at[t], qr.at[t]).wait()
                codes.append(jnp.transpose(kbuf[2 * t + core, pl.ds(D, D), :].astype(F32)))
            mine = qbuf[pl.ds(n_q * s, n_q)].reshape(n_q * tok, D).astype(F32) * SCALE
            code = jnp.concatenate(codes, axis=0) * weight
            query = jnp.concatenate([mine, code], axis=1).astype(BF)

            def mix(u, last):
                parts = []
                for j in range(n_k):
                    p = jnp.exp(jnp.dot(query, kbuf[n_k * u + j], preferred_element_type=F32))
                    if last:
                        p = jnp.where(key_at + j * tok <= query_at, p, 0.0)
                    parts.append(p.astype(BF))
                held = vbuf[pl.ds(n_k * u, n_k)].reshape(n_k * tok, 2 * D)
                return jnp.dot(jnp.concatenate(parts, axis=1), held, preferred_element_type=F32)

            acc[...] = mix(s, True)

            def earlier(u, c):
                acc[...] += mix(u, False)
                return c

            lax.fori_loop(0, s, earlier, 0)
            mixed = (acc[:, pl.ds(0, D)] / acc[:, pl.ds(D, D)]).astype(BF)
            obuf[pl.ds(n_q * s, n_q)] = mixed.reshape(n_q, tok, D)
            for j in range(n_q):
                t = n_q * s + j

                @pl.when(t == z)
                def _():
                    own_copy().start()

                @pl.when(t != z)
                def _():
                    o_copy(t).start()

            return carry

        lax.fori_loop(0, n_z // n_q, attend, 0)

        def done(i, c):
            t = lax.rem(z + i, n_z)
            v_pass(t).wait_send()
            k_pass(t).wait_send()

            @pl.when(t != z)
            def _():
                o_copy(t).wait_send()

            return c

        lax.fori_loop(0, n_z, done, 0)

    def o_wait(h, c):
        pltpu.make_async_copy(out_dst(h), out_dst(h), or_.at[h]).wait()
        return c

    lax.fori_loop(0, heads, o_wait, 0)

    def g_wait(c, carry):
        pltpu.make_async_copy(newc_ref.at[c], newc_ref.at[c], gr.at[c]).wait()
        return carry

    lax.fori_loop(0, n_ctx, g_wait, 0)

    def home_sent(h, c):
        sent_home(h, v_src(h), v_dst(me), vs, vr)
        sent_home(h, kst.at[h], k_dst(me), ks, kr)
        sent_home(h, q_src(h), qbuf.at[z], qs, qr)
        return c

    lax.fori_loop(0, heads, home_sent, 0)

    def ctx_sent(i, c):
        other = lax.rem(col + i, n_ctx)
        x_copy(other).wait_send()
        g_copy(other).wait_send()
        return c

    lax.fori_loop(1, n_ctx, ctx_sent, 0)

    def clu_sent(i, c):
        o = lax.rem(me + i, n_clu)
        z_copy(o).wait_send()
        f_copy(o).wait_send()
        return c

    lax.fori_loop(1, n_clu, clu_sent, 0)


def local(n_ctx, n_clu, queries, keys, values, clusters, centroids):
    tok, width = queries.shape
    heads = width // D
    n_z = n_clu // 2
    hbm = pl.BlockSpec(memory_space=pl.ANY)
    dma = pltpu.SemaphoreType.DMA
    attended, fresh = pl.pallas_call(
        functools.partial(kernel, n_ctx, n_clu),
        out_shape=(
            jax.ShapeDtypeStruct((tok, width), BF),
            jax.ShapeDtypeStruct((n_ctx, n_clu * heads, D), BF),
        ),
        in_specs=[hbm] * 5,
        out_specs=(hbm, hbm),
        scratch_shapes=[
            pltpu.VMEM((tok, width), BF),
            pltpu.VMEM((tok, width), BF),
            pltpu.VMEM((heads, tok), jnp.int32),
            pltpu.VMEM((n_ctx, heads, D), F32),
            pltpu.VMEM((heads, D + 16, tok), BF),
            pltpu.VMEM((heads, tok, 2 * D), BF),
            pltpu.VMEM((n_clu, 2 * D, tok), BF),
            pltpu.VMEM((n_clu, tok, 2 * D), BF),
            pltpu.VMEM((n_z, tok, D), BF),
            pltpu.VMEM((n_z, tok, D), BF),
            pltpu.VMEM((2 * tok, 2 * D), F32),
            pltpu.VMEM((n_ctx, heads, n_clu, D), BF),
            pltpu.VMEM((n_ctx, heads, n_clu, D), BF),
            pltpu.VMEM((n_clu * heads, D), F32),
            pltpu.VMEM((n_clu, heads, D), F32),
            pltpu.VMEM((n_clu, heads, D), F32),
            pltpu.VMEM((n_clu * heads, D), BF),
            dma((4,)),
            dma((heads,)),
            dma((n_z,)),
            dma((heads,)),
            dma((n_z,)),
            dma((heads,)),
            dma((n_z,)),
            dma((n_z,)),
            dma((n_z,)),
            dma((n_z,)),
            dma((n_z,)),
            dma((n_z,)),
            dma((heads,)),
            dma((n_ctx,)),
            dma((n_ctx,)),
            dma((n_clu,)),
            dma((n_clu,)),
            dma((n_clu,)),
            dma((n_clu,)),
            dma((n_ctx,)),
            dma((n_ctx,)),
        ],
        compiler_params=pltpu.CompilerParams(
            collective_id=0, has_side_effects=True, vmem_limit_bytes=40 * 1024 * 1024
        ),
        cost_estimate=pl.CostEstimate(
            flops=2 * 2 * 2 * D * tok * tok * n_clu * n_clu // 4,
            bytes_accessed=8 * tok * width,
            transcendentals=tok * tok * n_clu * n_clu // 4,
        ),
    )(queries, keys, values, clusters.T, centroids)
    fresh = jnp.swapaxes(fresh.reshape(n_ctx, n_clu, heads, D), 0, 1).astype(F32)
    return attended, fresh.reshape(n_clu * n_ctx, heads, D)


def solution(mesh):
    placed = (
        P(("ctx", "clu"), None),
        P(("ctx", "clu"), None),
        P(("ctx", "clu"), None),
        P(("ctx", "clu"), None),
        P("clu", None, None),
    )
    return jax.shard_map(
        functools.partial(local, mesh.shape["ctx"], mesh.shape["clu"]),
        mesh=mesh,
        in_specs=placed,
        out_specs=(P(("ctx", "clu"), None), P()),
        check_vma=False,
    )
```

```python
import functools
import math

import jax
import jax.numpy as jnp
from jax import lax
from jax.experimental import pallas as pl
from jax.experimental.pallas import tpu as pltpu
from jax.sharding import PartitionSpec as P

MESH = pl.DeviceIdType.MESH
EPS = 1e-06
SCALE = 8.0
DECAY = 0.75
D = 128
GAP = 64.0

BF = jnp.bfloat16
F32 = jnp.float32


def unit(rows):
    factor = lax.rsqrt(jnp.mean(rows * rows, axis=-1, keepdims=True) + EPS) / math.sqrt(D)
    return (rows * factor).astype(BF)


def kernel(
    n_ctx,
    n_clu,
    q_ref,
    k_ref,
    v_ref,
    clt_ref,
    cent_ref,
    out_ref,
    newc_ref,
    qin,
    kin,
    ids,
    cen,
    kst,
    nrm,
    kbuf,
    vbuf,
    qbuf,
    obuf,
    acc,
    sst,
    sin,
    zst,
    zsx,
    zsh,
    zin,
    fin,
    fnb,
    rel,
    relk,
    rr,
    rs,
    ls,
    vs,
    vr,
    ks,
    kr,
    qs,
    qr,
    ps,
    os_,
    or_,
    xs,
    xr,
    hs,
    zs,
    zr,
    fs,
    fr,
    gs,
    gr,
):
    tok = q_ref.shape[0]
    heads = q_ref.shape[1] // D
    n_z = n_clu // 2
    step = n_z // heads
    bits = max(1, (n_ctx * n_clu - 1).bit_length())

    col = lax.axis_index("ctx")
    me = lax.axis_index("clu")
    z = me // 2
    core = lax.rem(me, 2)
    sib = (col, me + 1 - 2 * core)
    is_home = lax.rem(z, step) == 0
    my_head = z // step
    opposite = lax.rem(z + n_z // 2, n_z)
    by_relay = lax.rem(z, 4) == 0
    relay_chip = lax.rem(z + n_z // 2 + 1, n_z)
    relay_from = lax.rem(z + n_z // 2 - 1, n_z)
    relay_to = lax.rem(z + n_z - 1, n_z)
    is_relay = lax.rem(relay_from, 4) == 0

    def spread(i, base, n):
        j = n - 1 - i
        off = jnp.where(lax.rem(j, 2) == 1, (j + 1) // 2, n - j // 2)
        return lax.rem(base + off, n)

    def remote(src, dst, send, recv, dev):
        return pltpu.make_async_remote_copy(
            src_ref=src, dst_ref=dst, send_sem=send, recv_sem=recv, device_id=dev, device_id_type=MESH
        )

    def lanes(h):
        return pl.ds(pl.multiple_of(h * D, D), D)

    def take(ref, sem):
        pltpu.make_async_copy(ref, ref, sem).wait()

    barrier = pltpu.get_barrier_semaphore()

    def greet_clu(i, c):
        pl.semaphore_signal(barrier, inc=1, device_id=(col, lax.rem(me + 2 * i, n_clu)), device_id_type=MESH)
        return c

    def greet_ctx(i, c):
        pl.semaphore_signal(barrier, inc=1, device_id=(lax.rem(col + i, n_ctx), me), device_id_type=MESH)
        return c

    loads = [
        pltpu.make_async_copy(src, dst, ls.at[i])
        for i, (src, dst) in enumerate(((k_ref, kin), (q_ref, qin), (clt_ref, ids), (cent_ref, cen)))
    ]
    for load in loads:
        load.start()
    pl.semaphore_signal(barrier, inc=1, device_id=sib, device_id_type=MESH)
    lax.fori_loop(1, n_z, greet_clu, 0)
    lax.fori_loop(1, n_ctx, greet_ctx, 0)
    pl.semaphore_wait(barrier, n_z + n_ctx - 1)

    def v_src(h):
        return v_ref.at[:, lanes(h)]

    def q_src(h):
        return nrm.at[h, :, pl.ds(0, D)]

    def q_all(n):
        return nrm.at[pl.ds(0, n), :, pl.ds(0, D)]

    def v_dst(c):
        return vbuf.at[c // 2, lax.rem(c, 2), :, pl.ds(0, D)]

    def k_dst(c):
        return kbuf.at[c // 2, lax.rem(c, 2), pl.ds(0, D + 16), :]

    def to_home(src, dst, send, recv, kind, h, start):
        target = h * step
        around = jnp.logical_and(by_relay, target == opposite)

        if start:

            @pl.when(target == z)
            def _():
                pltpu.make_async_copy(src, dst, recv).start()

        @pl.when(around)
        def _():
            held = relk if kind == 1 else rel.at[kind]
            copy = remote(src, held, send, rr.at[kind], (col, relay_chip * 2 + core))
            copy.start() if start else copy.wait_send()

        @pl.when(jnp.logical_and(target != z, jnp.logical_not(around)))
        def _():
            copy = remote(src, dst, send, recv, (col, target * 2 + core))
            copy.start() if start else copy.wait_send()

    def move_v(h, start):
        to_home(v_src(h), v_dst(me), vs.at[h], vr, 0, h, start)

    def move_k(h, start):
        to_home(kst.at[h], k_dst(me), ks.at[h], kr, 1, h, start)

    def move_q(h):
        to_home(q_src(h), qbuf.at[z], qs, qr.at[z], 2, h, True)

    def relay_copy(kind):
        c = 2 * relay_from + core
        held = relk if kind == 1 else rel.at[kind]
        dst, sem = (
            (v_dst(c), vr),
            (k_dst(c), kr),
            (qbuf.at[relay_from], qr.at[relay_from]),
            (out_ref.at[:, lanes(relay_from // step)], or_),
        )[kind]
        return remote(held, dst, rs.at[kind], sem, (col, relay_to * 2 + core))

    def relay(*kinds):
        @pl.when(is_relay)
        def _():
            for kind in kinds:
                held = relk if kind == 1 else rel.at[kind]
                pltpu.make_async_copy(held, held, rr.at[kind]).wait()
                relay_copy(kind).start()

    def send_v(i, c):
        h = spread(i, z // step, heads)
        move_v(h, True)
        return c

    lax.fori_loop(0, heads, send_v, 0)

    for load in loads:
        load.wait()

    row_id = lax.broadcasted_iota(jnp.int32, (16, tok), 0)

    def ready_head(i, c):
        h = spread(i, z // step, heads)
        kn = unit(kin[:, lanes(h)].astype(F32))
        qn = unit(qin[:, lanes(h)].astype(F32))
        nrm[h, :, pl.ds(0, D)] = qn
        nrm[h, :, pl.ds(D, D)] = kn
        kst[h, pl.ds(0, D), :] = jnp.transpose(kn.astype(F32)).astype(BF)
        row = jnp.broadcast_to(ids[pl.ds(h, 1), :], (16, tok))
        code = 2 * (lax.shift_right_logical(row, row_id) & 1) - 1
        code = jnp.where(row_id < bits, code, jnp.where(row_id == bits, 1, 0))
        kst[h, pl.ds(D, 16), :] = code.astype(F32).astype(BF)
        return c

    lax.fori_loop(0, heads, ready_head, 0)

    def send_k(i, c):
        h = spread(i, z // step, heads)
        move_v(h, False)
        move_k(h, True)
        return c

    def send_q(i, c):
        h = spread(i, z // step, heads)
        move_k(h, False)
        move_q(h)
        return c

    n_row = n_ctx * n_clu
    sum_row = lax.broadcasted_iota(jnp.int32, (n_row, tok), 0)

    def sum_head(h, c):
        row = ids[pl.ds(h, 1), :]
        owner = row // n_ctx
        place = lax.rem(row, n_ctx) * n_clu + lax.rem(owner, 2) * n_z + owner // 2
        pick = jnp.where(sum_row == place, 1.0, 0.0).astype(BF)
        both = jnp.dot(pick, nrm[h], preferred_element_type=F32)
        both = both[:, :D] + both[:, D:]
        sst[:, h, :, :] = both.reshape(n_ctx, n_clu, D).astype(BF)
        return c

    lax.fori_loop(0, heads, sum_head, 0)

    def x_copy(c):
        return remote(sst.at[c], sin.at[col], xs, xr, (c, me))

    def x_start(i, c):
        x_copy(lax.rem(col + i, n_ctx)).start()
        return c

    lax.fori_loop(1, n_ctx, x_start, 0)
    sin[col] = sst[col]

    @pl.when(is_home)
    def _():
        def fill(c, carry):
            vbuf[c // 2, lax.rem(c, 2), :, pl.ds(D, D)] = jnp.ones((tok, D), BF)
            kbuf[c // 2, lax.rem(c, 2), pl.ds(D + 16, D - 16), :] = jnp.zeros((D - 16, tok), BF)
            return carry

        lax.fori_loop(0, n_clu, fill, 0)

    lax.fori_loop(0, heads // 2, send_k, 0)
    take(sin.at[pl.ds(0, n_ctx - 1)], xr)
    for h in range(heads):
        part = sin[0, h].astype(F32)
        for c in range(1, n_ctx):
            part = part + sin[c, h].astype(F32)
        zst[pl.ds(h, n_clu, stride=heads), :] = part

    def half(c):
        return pl.ds(pl.multiple_of(c * n_z * heads, n_z * heads), n_z * heads)

    halves = remote(zst.at[half(1 - core)], zsx, hs.at[0], hs.at[1], sib)
    halves.start()
    halves.wait()
    zsh[...] = zst[half(core), :] + zsx[...]

    def z_rows(t):
        return pl.ds(pl.multiple_of(t * heads, heads), heads)

    def z_copy(t):
        return remote(zsh.at[z_rows(t)], zin.at[z], zs, zr, (col, 2 * t + core))

    def z_start(i, c):
        z_copy(lax.rem(z + i, n_z)).start()
        return c

    lax.fori_loop(1, n_z, z_start, 0)
    zin[z] = zsh[z_rows(z), :]
    lax.fori_loop(heads // 2, heads, send_k, 0)

    all_v = vbuf.at[:, core, :, pl.ds(0, D)]
    all_k = kbuf.at[:, core, pl.ds(0, D + 16), :]
    v_pass = remote(all_v, all_v, ps.at[0], ps.at[1], sib)
    k_pass = remote(all_k, all_k, ps.at[2], ps.at[3], sib)

    @pl.when(is_home)
    def _():
        take(all_v, vr)
        v_pass.start()

    relay(0)
    lax.fori_loop(0, heads // 2, send_q, 0)

    take(zin.at[pl.ds(0, n_z - 1)], zr)
    total = jnp.sum(zin[...], axis=0)
    fin[z] = DECAY * cen[col] + (1.0 - DECAY) / 2.0 * total

    def f_copy(t):
        return remote(fin.at[z], fin.at[z], fs, fr, (col, 2 * t + core))

    def f_start(i, c):
        f_copy(lax.rem(z + i, n_z)).start()
        return c

    lax.fori_loop(1, n_z, f_start, 0)
    lax.fori_loop(heads // 2, heads, send_q, 0)

    @pl.when(is_home)
    def _():
        take(all_k, kr)
        k_pass.start()

    relay(1)

    def g_copy(c):
        return remote(fnb, newc_ref.at[core, col], gs, gr, (c, me))

    def g_start(i, c):
        g_copy(lax.rem(col + i, n_ctx)).start()
        return c

    take(fin.at[pl.ds(0, n_z - 1)], fr)
    fnb[...] = fin[...].reshape(n_z * heads, D).astype(BF)
    lax.fori_loop(1, n_ctx, g_start, 0)
    pltpu.make_async_copy(fnb, newc_ref.at[core, col], gr).start()
    g_pass = remote(newc_ref.at[core], newc_ref.at[core], hs.at[2], hs.at[3], sib)

    def share():
        take(newc_ref.at[core], gr)
        g_pass.start()

    relay(2)

    @pl.when(jnp.logical_not(is_home))
    def _():
        share()

    relay(3)

    def out_dst(h):
        return out_ref.at[:, lanes(h)]

    def send_back(t):
        around = jnp.logical_and(by_relay, t == opposite)

        @pl.when(t == z)
        def _():
            pltpu.make_async_copy(obuf.at[t], out_dst(my_head), or_).start()

        @pl.when(around)
        def _():
            copy = remote(obuf.at[t], rel.at[3], os_, rr.at[3], (col, relay_chip * 2 + core))
            copy.start()

        @pl.when(jnp.logical_and(t != z, jnp.logical_not(around)))
        def _():
            copy = remote(obuf.at[t], out_dst(my_head), os_, or_, (col, 2 * t + core))
            copy.start()

    @pl.when(is_home)
    def _():
        v_pass.wait_recv()
        k_pass.wait_recv()

        n_q, n_k = 2, 4
        lane = lax.broadcasted_iota(jnp.int32, (n_q * tok, D), 1)
        weight = jnp.where(lane < bits, GAP, jnp.where(lane == bits, -GAP * bits, 0.0))
        key_at = lax.broadcasted_iota(jnp.int32, (n_q * tok, tok), 1)
        row_at = lax.broadcasted_iota(jnp.int32, (n_q * tok, tok), 0)
        query_at = (2 * (row_at // tok) + core) * tok + lax.rem(row_at, tok)

        def attend(i, carry):
            s = spread(i, z // n_q, n_z // n_q)
            codes = []
            for j in range(n_q):
                t = n_q * s + j
                pltpu.make_async_copy(qbuf.at[t], qbuf.at[t], qr.at[t]).wait()
                codes.append(jnp.transpose(kbuf[t, core, pl.ds(D, D), :].astype(F32)))
            mine = qbuf[pl.ds(n_q * s, n_q)].reshape(n_q * tok, D).astype(F32) * SCALE
            code = jnp.concatenate(codes, axis=0) * weight
            query = jnp.concatenate([mine, code], axis=1).astype(BF)

            def mix(u, last):
                parts = []
                for j in range(n_k):
                    p = jnp.exp(jnp.dot(query, kbuf[n_k // 2 * u + j // 2, j % 2], preferred_element_type=F32))
                    if last:
                        p = jnp.where(key_at + j * tok <= query_at, p, 0.0)
                    parts.append(p.astype(BF))
                held = vbuf[pl.ds(n_k // 2 * u, n_k // 2)].reshape(n_k * tok, 2 * D)
                return jnp.dot(jnp.concatenate(parts, axis=1), held, preferred_element_type=F32)

            acc[...] = mix(s, True)

            def earlier(u, c):
                acc[...] += mix(u, False)
                return c

            lax.fori_loop(0, s, earlier, 0)
            mixed = (acc[:, pl.ds(0, D)] / acc[:, pl.ds(D, D)]).astype(BF)
            obuf[pl.ds(n_q * s, n_q)] = mixed.reshape(n_q, tok, D)
            for j in range(n_q):
                send_back(n_q * s + j)

            @pl.when(i == n_z // n_q // 2)
            def _():
                share()

            return carry

        lax.fori_loop(0, n_z // n_q, attend, 0)

        v_pass.wait_send()
        k_pass.wait_send()
        take(obuf.at[pl.ds(0, n_z - 1)], os_)
        take(q_all(heads - 1), qs)

    @pl.when(jnp.logical_not(is_home))
    def _():
        take(q_all(heads), qs)

    @pl.when(is_relay)
    def _():
        for kind in range(4):
            relay_copy(kind).wait_send()

    take(sst.at[pl.ds(0, n_ctx - 1)], xs)
    take(zin.at[pl.ds(0, n_z - 1)], zs)
    take(fin.at[pl.ds(0, n_z - 1)], fs)
    take(newc_ref.at[core, pl.ds(0, n_ctx - 1)], gs)
    g_pass.wait()
    take(out_ref, or_)


def local(n_ctx, n_clu, queries, keys, values, clusters, centroids):
    tok, width = queries.shape
    heads = width // D
    n_z = n_clu // 2
    hbm = pl.BlockSpec(memory_space=pl.ANY)
    dma = pltpu.SemaphoreType.DMA
    attended, fresh = pl.pallas_call(
        functools.partial(kernel, n_ctx, n_clu),
        out_shape=(
            jax.ShapeDtypeStruct((tok, width), BF),
            jax.ShapeDtypeStruct((2, n_ctx, n_z * heads, D), BF),
        ),
        in_specs=[hbm] * 5,
        out_specs=(hbm, hbm),
        scratch_shapes=[
            pltpu.VMEM((tok, width), BF),
            pltpu.VMEM((tok, width), BF),
            pltpu.VMEM((heads, tok), jnp.int32),
            pltpu.VMEM((n_ctx, heads, D), F32),
            pltpu.VMEM((heads, D + 16, tok), BF),
            pltpu.VMEM((heads, tok, 2 * D), BF),
            pltpu.VMEM((n_z, 2, 2 * D, tok), BF),
            pltpu.VMEM((n_z, 2, tok, 2 * D), BF),
            pltpu.VMEM((n_z, tok, D), BF),
            pltpu.VMEM((n_z, tok, D), BF),
            pltpu.VMEM((2 * tok, 2 * D), F32),
            pltpu.VMEM((n_ctx, heads, n_clu, D), BF),
            pltpu.VMEM((n_ctx, heads, n_clu, D), BF),
            pltpu.VMEM((n_clu * heads, D), F32),
            pltpu.VMEM((n_z * heads, D), F32),
            pltpu.VMEM((n_z * heads, D), F32),
            pltpu.VMEM((n_z, heads, D), F32),
            pltpu.VMEM((n_z, heads, D), F32),
            pltpu.VMEM((n_z * heads, D), BF),
            pltpu.VMEM((4, tok, D), BF),
            pltpu.VMEM((D + 16, tok), BF),
            dma((4,)),
            dma((4,)),
            dma((4,)),
            dma((heads,)),
            dma(()),
            dma((heads,)),
            dma(()),
            dma(()),
            dma((n_z,)),
            dma((4,)),
            dma(()),
            dma(()),
            dma(()),
            dma(()),
            dma((4,)),
            dma(()),
            dma(()),
            dma(()),
            dma(()),
            dma(()),
            dma(()),
        ],
        compiler_params=pltpu.CompilerParams(
            collective_id=0, has_side_effects=True, vmem_limit_bytes=60 * 1024 * 1024
        ),
        cost_estimate=pl.CostEstimate(
            flops=2 * 2 * 2 * D * tok * tok * n_clu * n_clu // 4,
            bytes_accessed=8 * tok * width,
            transcendentals=tok * tok * n_clu * n_clu // 4,
        ),
    )(queries, keys, values, clusters.T, centroids)
    fresh = jnp.transpose(fresh.reshape(2, n_ctx, n_z, heads, D), (2, 0, 1, 3, 4)).astype(F32)
    return attended, fresh.reshape(n_clu * n_ctx, heads, D)


def solution(mesh):
    placed = (
        P(("ctx", "clu"), None),
        P(("ctx", "clu"), None),
        P(("ctx", "clu"), None),
        P(("ctx", "clu"), None),
        P("clu", None, None),
    )
    return jax.shard_map(
        functools.partial(local, mesh.shape["ctx"], mesh.shape["clu"]),
        mesh=mesh,
        in_specs=placed,
        out_specs=(P(("ctx", "clu"), None), P()),
        check_vma=False,
    )
```

```python
import functools
import math

import jax
import jax.numpy as jnp
from jax import lax
from jax.experimental import pallas as pl
from jax.experimental.pallas import tpu as pltpu
from jax.sharding import PartitionSpec as P

MESH = pl.DeviceIdType.MESH
EPS = 1e-06
SCALE = 8.0
DECAY = 0.75
D = 128
GAP = 64.0

BF = jnp.bfloat16
F32 = jnp.float32


def unit(rows):
    factor = lax.rsqrt(jnp.mean(rows * rows, axis=-1, keepdims=True) + EPS) / math.sqrt(D)
    return (rows * factor).astype(BF)


def kernel(
    n_ctx,
    n_clu,
    q_ref,
    k_ref,
    v_ref,
    clt_ref,
    cent_ref,
    out_ref,
    newc_ref,
    qin,
    kin,
    ids,
    cen,
    kst,
    nrm,
    kbuf,
    vbuf,
    qbuf,
    obuf,
    acc,
    sst,
    sin,
    zst,
    zsx,
    zsh,
    zin,
    fin,
    fnb,
    rel,
    relk,
    rr,
    rs,
    ls,
    vs,
    vr,
    ks,
    kr,
    qs,
    qr,
    ps,
    os_,
    or_,
    xs,
    xr,
    hs,
    zs,
    zr,
    fs,
    fr,
    gs,
    gr,
):
    tok = q_ref.shape[0]
    heads = q_ref.shape[1] // D
    n_z = n_clu // 2
    step = n_z // heads
    bits = max(1, (n_ctx * n_clu - 1).bit_length())

    col = lax.axis_index("ctx")
    me = lax.axis_index("clu")
    z = me // 2
    core = lax.rem(me, 2)
    sib = (col, me + 1 - 2 * core)
    is_home = lax.rem(z, step) == 0
    my_head = z // step
    opposite = lax.rem(z + n_z // 2, n_z)
    by_relay = lax.rem(z, 4) == 0
    relay_chip = lax.rem(z + n_z // 2 + 1, n_z)
    relay_from = lax.rem(z + n_z // 2 - 1, n_z)
    relay_to = lax.rem(z + n_z - 1, n_z)
    is_relay = lax.rem(relay_from, 4) == 0

    def spread(i, base, n):
        j = n - 1 - i
        off = jnp.where(lax.rem(j, 2) == 1, (j + 1) // 2, n - j // 2)
        return lax.rem(base + off, n)

    def remote(src, dst, send, recv, dev):
        return pltpu.make_async_remote_copy(
            src_ref=src, dst_ref=dst, send_sem=send, recv_sem=recv, device_id=dev, device_id_type=MESH
        )

    def lanes(h):
        return pl.ds(pl.multiple_of(h * D, D), D)

    def take(ref, sem):
        pltpu.make_async_copy(ref, ref, sem).wait()

    barrier = pltpu.get_barrier_semaphore()

    def greet_clu(i, c):
        pl.semaphore_signal(barrier, inc=1, device_id=(col, lax.rem(me + 2 * i, n_clu)), device_id_type=MESH)
        return c

    def greet_ctx(i, c):
        pl.semaphore_signal(barrier, inc=1, device_id=(lax.rem(col + i, n_ctx), me), device_id_type=MESH)
        return c

    loads = [
        pltpu.make_async_copy(src, dst, ls.at[i])
        for i, (src, dst) in enumerate(((k_ref, kin), (q_ref, qin), (clt_ref, ids), (cent_ref, cen)))
    ]
    for load in loads:
        load.start()
    pl.semaphore_signal(barrier, inc=1, device_id=sib, device_id_type=MESH)
    lax.fori_loop(1, n_z, greet_clu, 0)
    lax.fori_loop(1, n_ctx, greet_ctx, 0)
    pl.semaphore_wait(barrier, n_z + n_ctx - 1)

    def v_src(h):
        return v_ref.at[:, lanes(h)]

    def q_src(h):
        return nrm.at[h, :, pl.ds(0, D)]

    def q_all(n):
        return nrm.at[pl.ds(0, n), :, pl.ds(0, D)]

    def v_dst(c):
        return vbuf.at[c // 2, lax.rem(c, 2), :, pl.ds(0, D)]

    def k_dst(c):
        return kbuf.at[c // 2, lax.rem(c, 2), pl.ds(0, D + 16), :]

    def to_home(src, dst, send, recv, kind, h, start):
        target = h * step
        around = jnp.logical_and(by_relay, target == opposite)

        if start:

            @pl.when(target == z)
            def _():
                pltpu.make_async_copy(src, dst, recv).start()

        @pl.when(around)
        def _():
            held = relk if kind == 1 else rel.at[kind]
            copy = remote(src, held, send, rr.at[kind], (col, relay_chip * 2 + core))
            copy.start() if start else copy.wait_send()

        @pl.when(jnp.logical_and(target != z, jnp.logical_not(around)))
        def _():
            copy = remote(src, dst, send, recv, (col, target * 2 + core))
            copy.start() if start else copy.wait_send()

    def move_v(h, start):
        to_home(v_src(h), v_dst(me), vs.at[h], vr, 0, h, start)

    def move_k(h, start):
        to_home(kst.at[h], k_dst(me), ks.at[h], kr, 1, h, start)

    def move_q(h):
        to_home(q_src(h), qbuf.at[z], qs, qr.at[z], 2, h, True)

    def relay_copy(kind):
        c = 2 * relay_from + core
        held = relk if kind == 1 else rel.at[kind]
        dst, sem = (
            (v_dst(c), vr),
            (k_dst(c), kr),
            (qbuf.at[relay_from], qr.at[relay_from]),
            (out_ref.at[:, lanes(relay_from // step)], or_),
        )[kind]
        return remote(held, dst, rs.at[kind], sem, (col, relay_to * 2 + core))

    def relay(*kinds):
        @pl.when(is_relay)
        def _():
            for kind in kinds:
                held = relk if kind == 1 else rel.at[kind]
                pltpu.make_async_copy(held, held, rr.at[kind]).wait()
                relay_copy(kind).start()

    def send_v(i, c):
        h = spread(i, z // step, heads)
        move_v(h, True)
        return c

    lax.fori_loop(0, heads, send_v, 0)

    for load in loads:
        load.wait()

    row_id = lax.broadcasted_iota(jnp.int32, (16, tok), 0)

    def ready_head(i, c):
        h = spread(i, z // step, heads)
        kn = unit(kin[:, lanes(h)].astype(F32))
        qn = unit(qin[:, lanes(h)].astype(F32))
        nrm[h, :, pl.ds(0, D)] = qn
        nrm[h, :, pl.ds(D, D)] = kn
        kst[h, pl.ds(0, D), :] = jnp.transpose(kn.astype(F32)).astype(BF)
        row = jnp.broadcast_to(ids[pl.ds(h, 1), :], (16, tok))
        code = 2 * (lax.shift_right_logical(row, row_id) & 1) - 1
        code = jnp.where(row_id < bits, code, jnp.where(row_id == bits, 1, 0))
        kst[h, pl.ds(D, 16), :] = code.astype(F32).astype(BF)
        return c

    lax.fori_loop(0, heads, ready_head, 0)

    def send_k(i, c):
        h = spread(i, z // step, heads)
        move_v(h, False)
        move_k(h, True)
        return c

    def send_q(i, c):
        h = spread(i, z // step, heads)
        move_k(h, False)
        move_q(h)
        return c

    n_row = n_ctx * n_clu
    sum_row = lax.broadcasted_iota(jnp.int32, (n_row, tok), 0)

    def sum_head(h, c):
        row = ids[pl.ds(h, 1), :]
        owner = row // n_ctx
        place = lax.rem(row, n_ctx) * n_clu + lax.rem(owner, 2) * n_z + owner // 2
        pick = jnp.where(sum_row == place, 1.0, 0.0).astype(BF)
        both = jnp.dot(pick, nrm[h], preferred_element_type=F32)
        both = both[:, :D] + both[:, D:]
        sst[:, h, :, :] = both.reshape(n_ctx, n_clu, D).astype(BF)
        return c

    lax.fori_loop(0, heads, sum_head, 0)

    def x_copy(c):
        return remote(sst.at[c], sin.at[col], xs, xr, (c, me))

    def x_start(i, c):
        x_copy(lax.rem(col + i, n_ctx)).start()
        return c

    lax.fori_loop(1, n_ctx, x_start, 0)
    sin[col] = sst[col]

    @pl.when(is_home)
    def _():
        def fill(c, carry):
            vbuf[c // 2, lax.rem(c, 2), :, pl.ds(D, D)] = jnp.ones((tok, D), BF)
            kbuf[c // 2, lax.rem(c, 2), pl.ds(D + 16, D - 16), :] = jnp.zeros((D - 16, tok), BF)
            return carry

        lax.fori_loop(0, n_clu, fill, 0)

    lax.fori_loop(0, heads // 2, send_k, 0)
    take(sin.at[pl.ds(0, n_ctx - 1)], xr)
    for h in range(heads):
        part = sin[0, h].astype(F32)
        for c in range(1, n_ctx):
            part = part + sin[c, h].astype(F32)
        zst[pl.ds(h, n_clu, stride=heads), :] = part

    def half(c):
        return pl.ds(pl.multiple_of(c * n_z * heads, n_z * heads), n_z * heads)

    halves = remote(zst.at[half(1 - core)], zsx, hs.at[0], hs.at[1], sib)
    halves.start()
    halves.wait()
    zsh[...] = zst[half(core), :] + zsx[...]

    def z_rows(t):
        return pl.ds(pl.multiple_of(t * heads, heads), heads)

    def z_copy(t):
        return remote(zsh.at[z_rows(t)], zin.at[z], zs, zr, (col, 2 * t + core))

    def z_start(i, c):
        z_copy(lax.rem(z + i, n_z)).start()
        return c

    lax.fori_loop(1, n_z, z_start, 0)
    zin[z] = zsh[z_rows(z), :]
    lax.fori_loop(heads // 2, heads, send_k, 0)

    all_v = vbuf.at[:, core, :, pl.ds(0, D)]
    all_k = kbuf.at[:, core, pl.ds(0, D + 16), :]
    v_pass = remote(all_v, all_v, ps.at[0], ps.at[1], sib)
    k_pass = remote(all_k, all_k, ps.at[2], ps.at[3], sib)

    @pl.when(is_home)
    def _():
        take(all_v, vr)
        v_pass.start()

    relay(0)
    lax.fori_loop(0, heads // 2, send_q, 0)

    take(zin.at[pl.ds(0, n_z - 1)], zr)
    total = jnp.sum(zin[...], axis=0)
    fin[z] = DECAY * cen[col] + (1.0 - DECAY) / 2.0 * total

    def f_copy(t):
        return remote(fin.at[z], fin.at[z], fs, fr, (col, 2 * t + core))

    def f_start(i, c):
        f_copy(lax.rem(z + i, n_z)).start()
        return c

    lax.fori_loop(1, n_z, f_start, 0)
    lax.fori_loop(heads // 2, heads, send_q, 0)

    @pl.when(is_home)
    def _():
        take(all_k, kr)
        k_pass.start()

    relay(1, 2)

    def g_copy(c):
        return remote(fnb, newc_ref.at[core, col], gs, gr, (c, me))

    def g_start(i, c):
        g_copy(lax.rem(col + i, n_ctx)).start()
        return c

    take(fin.at[pl.ds(0, n_z - 1)], fr)
    fnb[...] = fin[...].reshape(n_z * heads, D).astype(BF)
    lax.fori_loop(1, n_ctx, g_start, 0)
    pltpu.make_async_copy(fnb, newc_ref.at[core, col], gr).start()
    g_pass = remote(newc_ref.at[core], newc_ref.at[core], hs.at[2], hs.at[3], sib)

    def share():
        take(newc_ref.at[core], gr)
        g_pass.start()

    @pl.when(jnp.logical_not(is_home))
    def _():
        share()

    relay(3)

    def out_dst(h):
        return out_ref.at[:, lanes(h)]

    def send_back(t):
        around = jnp.logical_and(by_relay, t == opposite)

        @pl.when(t == z)
        def _():
            pltpu.make_async_copy(obuf.at[t], out_dst(my_head), or_).start()

        @pl.when(around)
        def _():
            copy = remote(obuf.at[t], rel.at[3], os_, rr.at[3], (col, relay_chip * 2 + core))
            copy.start()

        @pl.when(jnp.logical_and(t != z, jnp.logical_not(around)))
        def _():
            copy = remote(obuf.at[t], out_dst(my_head), os_, or_, (col, 2 * t + core))
            copy.start()

    @pl.when(is_home)
    def _():
        v_pass.wait_recv()
        k_pass.wait_recv()

        n_q = 2
        lane = lax.broadcasted_iota(jnp.int32, (n_q * tok, D), 1)
        weight = jnp.where(lane < bits, GAP, jnp.where(lane == bits, -GAP * bits, 0.0))
        key_at = lax.broadcasted_iota(jnp.int32, (n_q * tok, tok), 1)
        row_at = lax.broadcasted_iota(jnp.int32, (n_q * tok, tok), 0)
        query_at = (2 * (row_at // tok) + core) * tok + lax.rem(row_at, tok)

        def attend(i, carry):
            s = spread(jnp.where(i < 3, lax.rem(i + 1, 3), i), z // n_q, n_z // n_q)
            codes = []
            for j in range(n_q):
                t = n_q * s + j
                pltpu.make_async_copy(qbuf.at[t], qbuf.at[t], qr.at[t]).wait()
                codes.append(jnp.transpose(kbuf[t, core, pl.ds(D, D), :].astype(F32)))
            mine = qbuf[pl.ds(n_q * s, n_q)].reshape(n_q * tok, D).astype(F32) * SCALE
            code = jnp.concatenate(codes, axis=0) * weight
            query = jnp.concatenate([mine, code], axis=1).astype(BF)

            def weigh(rows, t, c, causal):
                p = jnp.exp(jnp.dot(query[rows], kbuf[t, c], preferred_element_type=F32))
                if causal:
                    p = jnp.where(key_at[rows] + (2 * (t - n_q * s) + c) * tok <= query_at[rows], p, 0.0)
                return p.astype(BF)

            def mix(rows, t, n, causal):
                parts = [
                    weigh(rows, t + k, c, causal and k == n - 1) for k in range(n) for c in range(2)
                ]
                held = vbuf[pl.ds(t, n)].reshape(2 * n * tok, 2 * D)
                return jnp.dot(jnp.concatenate(parts, axis=1), held, preferred_element_type=F32)

            every = slice(0, n_q * tok)
            for j in range(n_q):
                rows = slice(j * tok, (j + 1) * tok)
                acc[rows, :] = mix(rows, n_q * s, j + 1, True)

            @pl.when(lax.rem(s, 2) == 1)
            def _():
                acc[...] += mix(every, n_q * (s - 1), n_q, False)

            def earlier(u, c):
                acc[...] += mix(every, 2 * n_q * u, 2 * n_q, False)
                return c

            lax.fori_loop(0, s // 2, earlier, 0)
            mixed = (acc[:, pl.ds(0, D)] / acc[:, pl.ds(D, D)]).astype(BF)
            obuf[pl.ds(n_q * s, n_q)] = mixed.reshape(n_q, tok, D)
            for j in range(n_q):
                send_back(n_q * s + j)

            @pl.when(i == n_z // n_q // 2)
            def _():
                share()

            return carry

        lax.fori_loop(0, n_z // n_q, attend, 0)

        v_pass.wait_send()
        k_pass.wait_send()
        take(obuf.at[pl.ds(0, n_z - 1)], os_)
        take(q_all(heads - 1), qs)

    @pl.when(jnp.logical_not(is_home))
    def _():
        take(q_all(heads), qs)

    @pl.when(is_relay)
    def _():
        for kind in range(4):
            relay_copy(kind).wait_send()

    take(sst.at[pl.ds(0, n_ctx - 1)], xs)
    take(zin.at[pl.ds(0, n_z - 1)], zs)
    take(fin.at[pl.ds(0, n_z - 1)], fs)
    take(newc_ref.at[core, pl.ds(0, n_ctx - 1)], gs)
    g_pass.wait()
    take(out_ref, or_)


def local(n_ctx, n_clu, queries, keys, values, clusters, centroids):
    tok, width = queries.shape
    heads = width // D
    n_z = n_clu // 2
    hbm = pl.BlockSpec(memory_space=pl.ANY)
    dma = pltpu.SemaphoreType.DMA
    attended, fresh = pl.pallas_call(
        functools.partial(kernel, n_ctx, n_clu),
        out_shape=(
            jax.ShapeDtypeStruct((tok, width), BF),
            jax.ShapeDtypeStruct((2, n_ctx, n_z * heads, D), BF),
        ),
        in_specs=[hbm] * 5,
        out_specs=(hbm, hbm),
        scratch_shapes=[
            pltpu.VMEM((tok, width), BF),
            pltpu.VMEM((tok, width), BF),
            pltpu.VMEM((heads, tok), jnp.int32),
            pltpu.VMEM((n_ctx, heads, D), F32),
            pltpu.VMEM((heads, D + 16, tok), BF),
            pltpu.VMEM((heads, tok, 2 * D), BF),
            pltpu.VMEM((n_z, 2, 2 * D, tok), BF),
            pltpu.VMEM((n_z, 2, tok, 2 * D), BF),
            pltpu.VMEM((n_z, tok, D), BF),
            pltpu.VMEM((n_z, tok, D), BF),
            pltpu.VMEM((2 * tok, 2 * D), F32),
            pltpu.VMEM((n_ctx, heads, n_clu, D), BF),
            pltpu.VMEM((n_ctx, heads, n_clu, D), BF),
            pltpu.VMEM((n_clu * heads, D), F32),
            pltpu.VMEM((n_z * heads, D), F32),
            pltpu.VMEM((n_z * heads, D), F32),
            pltpu.VMEM((n_z, heads, D), F32),
            pltpu.VMEM((n_z, heads, D), F32),
            pltpu.VMEM((n_z * heads, D), BF),
            pltpu.VMEM((4, tok, D), BF),
            pltpu.VMEM((D + 16, tok), BF),
            dma((4,)),
            dma((4,)),
            dma((4,)),
            dma((heads,)),
            dma(()),
            dma((heads,)),
            dma(()),
            dma(()),
            dma((n_z,)),
            dma((4,)),
            dma(()),
            dma(()),
            dma(()),
            dma(()),
            dma((4,)),
            dma(()),
            dma(()),
            dma(()),
            dma(()),
            dma(()),
            dma(()),
        ],
        compiler_params=pltpu.CompilerParams(
            collective_id=0, has_side_effects=True, vmem_limit_bytes=60 * 1024 * 1024
        ),
        cost_estimate=pl.CostEstimate(
            flops=2 * 2 * 2 * D * tok * tok * n_clu * n_clu // 4,
            bytes_accessed=8 * tok * width,
            transcendentals=tok * tok * n_clu * n_clu // 4,
        ),
    )(queries, keys, values, clusters.T, centroids)
    fresh = jnp.transpose(fresh.reshape(2, n_ctx, n_z, heads, D), (2, 0, 1, 3, 4)).astype(F32)
    return attended, fresh.reshape(n_clu * n_ctx, heads, D)


def solution(mesh):
    placed = (
        P(("ctx", "clu"), None),
        P(("ctx", "clu"), None),
        P(("ctx", "clu"), None),
        P(("ctx", "clu"), None),
        P("clu", None, None),
    )
    return jax.shard_map(
        functools.partial(local, mesh.shape["ctx"], mesh.shape["clu"]),
        mesh=mesh,
        in_specs=placed,
        out_specs=(P(("ctx", "clu"), None), P()),
        check_vma=False,
    )
```

```python
import functools
import math

import jax
import jax.numpy as jnp
from jax import lax
from jax.experimental import pallas as pl
from jax.experimental.pallas import tpu as pltpu
from jax.sharding import PartitionSpec as P

MESH = pl.DeviceIdType.MESH
EPS = 1e-06
SCALE = 8.0
DECAY = 0.75
D = 128
GAP = 64.0

BF = jnp.bfloat16
F32 = jnp.float32


def unit(rows):
    factor = lax.rsqrt(jnp.mean(rows * rows, axis=-1, keepdims=True) + EPS) / math.sqrt(D)
    return (rows * factor).astype(BF)


def kernel(
    n_ctx,
    n_clu,
    q_ref,
    k_ref,
    v_ref,
    clt_ref,
    cent_ref,
    out_ref,
    newc_ref,
    qin,
    kin,
    ids,
    cen,
    kst,
    nrm,
    kbuf,
    vbuf,
    qbuf,
    obuf,
    acc,
    sst,
    sin,
    zst,
    zsx,
    zsh,
    zin,
    fin,
    fnb,
    rel,
    relk,
    rr,
    rs,
    ls,
    vs,
    vr,
    ks,
    kr,
    qs,
    qr,
    ps,
    os_,
    or_,
    xs,
    xr,
    hs,
    zs,
    zr,
    fs,
    fr,
    gs,
    gr,
):
    tok = q_ref.shape[0]
    heads = q_ref.shape[1] // D
    n_z = n_clu // 2
    step = n_z // heads
    bits = max(1, (n_ctx * n_clu - 1).bit_length())

    col = lax.axis_index("ctx")
    me = lax.axis_index("clu")
    z = me // 2
    core = lax.rem(me, 2)
    sib = (col, me + 1 - 2 * core)
    is_home = lax.rem(z, step) == 0
    my_head = z // step
    opposite = lax.rem(z + n_z // 2, n_z)
    by_relay = lax.rem(z, 4) == 0
    relay_chip = lax.rem(z + n_z // 2 + 1, n_z)
    relay_from = lax.rem(z + n_z // 2 - 1, n_z)
    relay_to = lax.rem(z + n_z - 1, n_z)
    is_relay = lax.rem(relay_from, 4) == 0

    def spread(i, base, n):
        j = n - 1 - i
        off = jnp.where(lax.rem(j, 2) == 1, (j + 1) // 2, n - j // 2)
        return lax.rem(base + off, n)

    def remote(src, dst, send, recv, dev):
        return pltpu.make_async_remote_copy(
            src_ref=src, dst_ref=dst, send_sem=send, recv_sem=recv, device_id=dev, device_id_type=MESH
        )

    def lanes(h):
        return pl.ds(pl.multiple_of(h * D, D), D)

    def take(ref, sem):
        pltpu.make_async_copy(ref, ref, sem).wait()

    barrier = pltpu.get_barrier_semaphore()

    def greet_clu(i, c):
        pl.semaphore_signal(barrier, inc=1, device_id=(col, lax.rem(me + 2 * i, n_clu)), device_id_type=MESH)
        return c

    def greet_ctx(i, c):
        pl.semaphore_signal(barrier, inc=1, device_id=(lax.rem(col + i, n_ctx), me), device_id_type=MESH)
        return c

    loads = [
        pltpu.make_async_copy(src, dst, ls.at[i])
        for i, (src, dst) in enumerate(((k_ref, kin), (q_ref, qin), (clt_ref, ids), (cent_ref, cen)))
    ]
    for load in loads:
        load.start()
    pl.semaphore_signal(barrier, inc=1, device_id=sib, device_id_type=MESH)
    lax.fori_loop(1, n_z, greet_clu, 0)
    lax.fori_loop(1, n_ctx, greet_ctx, 0)
    pl.semaphore_wait(barrier, n_z + n_ctx - 1)

    def v_src(h):
        return v_ref.at[:, lanes(h)]

    def q_src(h):
        return nrm.at[h, :, pl.ds(0, D)]

    def q_all(n):
        return nrm.at[pl.ds(0, n), :, pl.ds(0, D)]

    def v_dst(c):
        return vbuf.at[c // 2, lax.rem(c, 2), :, pl.ds(0, D)]

    def k_dst(c):
        return kbuf.at[c // 2, lax.rem(c, 2), pl.ds(0, D + 16), :]

    def to_home(src, dst, send, recv, kind, h, start):
        target = h * step
        around = jnp.logical_and(by_relay, target == opposite)

        if start:

            @pl.when(target == z)
            def _():
                pltpu.make_async_copy(src, dst, recv).start()

        @pl.when(around)
        def _():
            held = relk if kind == 1 else rel.at[kind]
            copy = remote(src, held, send, rr.at[kind], (col, relay_chip * 2 + core))
            copy.start() if start else copy.wait_send()

        @pl.when(jnp.logical_and(target != z, jnp.logical_not(around)))
        def _():
            copy = remote(src, dst, send, recv, (col, target * 2 + core))
            copy.start() if start else copy.wait_send()

    def move_v(h, start):
        to_home(v_src(h), v_dst(me), vs.at[h], vr, 0, h, start)

    def move_k(h, start):
        to_home(kst.at[h], k_dst(me), ks.at[h], kr, 1, h, start)

    def move_q(h):
        to_home(q_src(h), qbuf.at[z], qs, qr.at[z], 2, h, True)

    def relay_copy(kind):
        c = 2 * relay_from + core
        held = relk if kind == 1 else rel.at[kind]
        dst, sem = (
            (v_dst(c), vr),
            (k_dst(c), kr),
            (qbuf.at[relay_from], qr.at[relay_from]),
            (out_ref.at[:, lanes(relay_from // step)], or_),
        )[kind]
        return remote(held, dst, rs.at[kind], sem, (col, relay_to * 2 + core))

    def relay(*kinds):
        @pl.when(is_relay)
        def _():
            for kind in kinds:
                held = relk if kind == 1 else rel.at[kind]
                pltpu.make_async_copy(held, held, rr.at[kind]).wait()
                relay_copy(kind).start()

    def send_v(i, c):
        h = spread(i, z // step, heads)
        move_v(h, True)
        return c

    lax.fori_loop(0, heads, send_v, 0)

    for load in loads:
        load.wait()

    row_id = lax.broadcasted_iota(jnp.int32, (16, tok), 0)

    def ready_head(i, c):
        h = spread(i, z // step, heads)
        kn = unit(kin[:, lanes(h)].astype(F32))
        qn = unit(qin[:, lanes(h)].astype(F32))
        nrm[h, :, pl.ds(0, D)] = qn
        nrm[h, :, pl.ds(D, D)] = kn
        kst[h, pl.ds(0, D), :] = jnp.transpose(kn.astype(F32)).astype(BF)
        row = jnp.broadcast_to(ids[pl.ds(h, 1), :], (16, tok))
        code = 2 * (lax.shift_right_logical(row, row_id) & 1) - 1
        code = jnp.where(row_id < bits, code, jnp.where(row_id == bits, 1, 0))
        kst[h, pl.ds(D, 16), :] = code.astype(F32).astype(BF)
        return c

    lax.fori_loop(0, heads, ready_head, 0)

    def send_k(i, c):
        h = spread(i, z // step, heads)
        move_v(h, False)
        move_k(h, True)
        return c

    def send_q(i, c):
        move_q(spread(i, z // step, heads))
        return c

    n_row = n_ctx * n_clu
    sum_row = lax.broadcasted_iota(jnp.int32, (n_row, tok), 0)

    def sum_head(h, c):
        row = ids[pl.ds(h, 1), :]
        owner = row // n_ctx
        place = lax.rem(row, n_ctx) * n_clu + lax.rem(owner, 2) * n_z + owner // 2
        pick = jnp.where(sum_row == place, 1.0, 0.0).astype(BF)
        both = jnp.dot(pick, nrm[h], preferred_element_type=F32)
        both = both[:, :D] + both[:, D:]
        sst[:, h, :, :] = both.reshape(n_ctx, n_clu, D).astype(BF)
        return c

    lax.fori_loop(0, heads, sum_head, 0)

    def x_copy(c):
        return remote(sst.at[c], sin.at[col], xs, xr, (c, me))

    def x_start(i, c):
        x_copy(lax.rem(col + i, n_ctx)).start()
        return c

    lax.fori_loop(1, n_ctx, x_start, 0)
    sin[col] = sst[col]

    @pl.when(is_home)
    def _():
        def fill(c, carry):
            vbuf[c // 2, lax.rem(c, 2), :, pl.ds(D, D)] = jnp.ones((tok, D), BF)
            kbuf[c // 2, lax.rem(c, 2), pl.ds(D + 16, D - 16), :] = jnp.zeros((D - 16, tok), BF)
            return carry

        lax.fori_loop(0, n_clu, fill, 0)

    lax.fori_loop(0, heads // 2, send_k, 0)
    take(sin.at[pl.ds(0, n_ctx - 1)], xr)
    for h in range(heads):
        part = sin[0, h].astype(F32)
        for c in range(1, n_ctx):
            part = part + sin[c, h].astype(F32)
        zst[pl.ds(h, n_clu, stride=heads), :] = part

    def half(c):
        return pl.ds(pl.multiple_of(c * n_z * heads, n_z * heads), n_z * heads)

    halves = remote(zst.at[half(1 - core)], zsx, hs.at[0], hs.at[1], sib)
    halves.start()
    halves.wait()
    zsh[...] = zst[half(core), :] + zsx[...]

    def z_rows(t):
        return pl.ds(pl.multiple_of(t * heads, heads), heads)

    def z_copy(t):
        return remote(zsh.at[z_rows(t)], zin.at[z], zs, zr, (col, 2 * t + core))

    def z_start(i, c):
        z_copy(lax.rem(z + i, n_z)).start()
        return c

    lax.fori_loop(1, n_z, z_start, 0)
    zin[z] = zsh[z_rows(z), :]
    lax.fori_loop(heads // 2, heads, send_k, 0)

    all_v = vbuf.at[:, core, :, pl.ds(0, D)]
    all_k = kbuf.at[:, core, pl.ds(0, D + 16), :]
    v_pass = remote(all_v, all_v, ps.at[0], ps.at[1], sib)
    k_pass = remote(all_k, all_k, ps.at[2], ps.at[3], sib)

    @pl.when(is_home)
    def _():
        take(all_v, vr)
        v_pass.start()

    relay(0)
    lax.fori_loop(0, heads // 2, send_q, 0)

    take(zin.at[pl.ds(0, n_z - 1)], zr)
    total = jnp.sum(zin[...], axis=0)
    fin[z] = DECAY * cen[col] + (1.0 - DECAY) / 2.0 * total

    def f_copy(t):
        return remote(fin.at[z], fin.at[z], fs, fr, (col, 2 * t + core))

    def f_start(i, c):
        f_copy(lax.rem(z + i, n_z)).start()
        return c

    lax.fori_loop(1, n_z, f_start, 0)
    lax.fori_loop(heads // 2, heads, send_q, 0)

    @pl.when(is_home)
    def _():
        take(all_k, kr)
        k_pass.start()

    relay(1, 2)

    def g_copy(c):
        return remote(fnb, newc_ref.at[core, col], gs, gr, (c, me))

    def g_start(i, c):
        g_copy(lax.rem(col + i, n_ctx)).start()
        return c

    take(fin.at[pl.ds(0, n_z - 1)], fr)
    fnb[...] = fin[...].reshape(n_z * heads, D).astype(BF)
    lax.fori_loop(1, n_ctx, g_start, 0)
    pltpu.make_async_copy(fnb, newc_ref.at[core, col], gr).start()
    g_pass = remote(newc_ref.at[core], newc_ref.at[core], hs.at[2], hs.at[3], sib)

    def share():
        take(newc_ref.at[core], gr)
        g_pass.start()

    @pl.when(jnp.logical_not(is_home))
    def _():
        share()

    relay(3)

    def out_dst(h):
        return out_ref.at[:, lanes(h)]

    def send_back(t):
        around = jnp.logical_and(by_relay, t == opposite)

        @pl.when(t == z)
        def _():
            pltpu.make_async_copy(obuf.at[t], out_dst(my_head), or_).start()

        @pl.when(around)
        def _():
            copy = remote(obuf.at[t], rel.at[3], os_, rr.at[3], (col, relay_chip * 2 + core))
            copy.start()

        @pl.when(jnp.logical_and(t != z, jnp.logical_not(around)))
        def _():
            copy = remote(obuf.at[t], out_dst(my_head), os_, or_, (col, 2 * t + core))
            copy.start()

    @pl.when(is_home)
    def _():
        v_pass.wait_recv()
        k_pass.wait_recv()

        n_q = 2
        lane = lax.broadcasted_iota(jnp.int32, (n_q * tok, D), 1)
        weight = jnp.where(lane < bits, GAP, jnp.where(lane == bits, -GAP * bits, 0.0))
        key_at = lax.broadcasted_iota(jnp.int32, (n_q * tok, tok), 1)
        row_at = lax.broadcasted_iota(jnp.int32, (n_q * tok, tok), 0)
        query_at = (2 * (row_at // tok) + core) * tok + lax.rem(row_at, tok)

        def attend(i, carry):
            s = spread(jnp.where(i < 3, lax.rem(i + 1, 3), i), z // n_q, n_z // n_q)
            codes = []
            for j in range(n_q):
                t = n_q * s + j
                pltpu.make_async_copy(qbuf.at[t], qbuf.at[t], qr.at[t]).wait()
                codes.append(jnp.transpose(kbuf[t, core, pl.ds(D, D), :].astype(F32)))
            mine = qbuf[pl.ds(n_q * s, n_q)].reshape(n_q * tok, D).astype(F32) * SCALE
            code = jnp.concatenate(codes, axis=0) * weight
            query = jnp.concatenate([mine, code], axis=1).astype(BF)

            def weigh(rows, t, c, causal):
                p = jnp.exp(jnp.dot(query[rows], kbuf[t, c], preferred_element_type=F32))
                if causal:
                    p = jnp.where(key_at[rows] + (2 * (t - n_q * s) + c) * tok <= query_at[rows], p, 0.0)
                return p.astype(BF)

            def mix(rows, t, n, causal):
                parts = [
                    weigh(rows, t + k, c, causal and k == n - 1) for k in range(n) for c in range(2)
                ]
                held = vbuf[pl.ds(t, n)].reshape(2 * n * tok, 2 * D)
                return jnp.dot(jnp.concatenate(parts, axis=1), held, preferred_element_type=F32)

            every = slice(0, n_q * tok)
            for j in range(n_q):
                rows = slice(j * tok, (j + 1) * tok)
                acc[rows, :] = mix(rows, n_q * s, j + 1, True)

            run = 1
            while run < n_z // n_q:

                @pl.when(lax.rem(s // run, 2) == 1)
                def _(run=run):
                    acc[...] += mix(every, n_q * (s // (2 * run)) * 2 * run, n_q * run, False)

                run *= 2

            mixed = (acc[:, pl.ds(0, D)] / acc[:, pl.ds(D, D)]).astype(BF)
            obuf[pl.ds(n_q * s, n_q)] = mixed.reshape(n_q, tok, D)
            for j in range(n_q):
                send_back(n_q * s + j)

            @pl.when(i == n_z // n_q // 2)
            def _():
                share()

            return carry

        lax.fori_loop(0, n_z // n_q, attend, 0)

        v_pass.wait_send()
        k_pass.wait_send()
        take(obuf.at[pl.ds(0, n_z - 1)], os_)
        take(q_all(heads - 1), qs)

    @pl.when(jnp.logical_not(is_home))
    def _():
        take(q_all(heads), qs)

    @pl.when(is_relay)
    def _():
        for kind in range(4):
            relay_copy(kind).wait_send()

    def keys_left(h, c):
        move_k(h, False)
        return c

    lax.fori_loop(0, heads, keys_left, 0)
    take(sst.at[pl.ds(0, n_ctx - 1)], xs)
    take(zin.at[pl.ds(0, n_z - 1)], zs)
    take(fin.at[pl.ds(0, n_z - 1)], fs)
    take(newc_ref.at[core, pl.ds(0, n_ctx - 1)], gs)
    g_pass.wait()
    take(out_ref, or_)


def local(n_ctx, n_clu, queries, keys, values, clusters, centroids):
    tok, width = queries.shape
    heads = width // D
    n_z = n_clu // 2
    hbm = pl.BlockSpec(memory_space=pl.ANY)
    dma = pltpu.SemaphoreType.DMA
    attended, fresh = pl.pallas_call(
        functools.partial(kernel, n_ctx, n_clu),
        out_shape=(
            jax.ShapeDtypeStruct((tok, width), BF),
            jax.ShapeDtypeStruct((2, n_ctx, n_z * heads, D), BF),
        ),
        in_specs=[hbm] * 5,
        out_specs=(hbm, hbm),
        scratch_shapes=[
            pltpu.VMEM((tok, width), BF),
            pltpu.VMEM((tok, width), BF),
            pltpu.VMEM((heads, tok), jnp.int32),
            pltpu.VMEM((n_ctx, heads, D), F32),
            pltpu.VMEM((heads, D + 16, tok), BF),
            pltpu.VMEM((heads, tok, 2 * D), BF),
            pltpu.VMEM((n_z, 2, 2 * D, tok), BF),
            pltpu.VMEM((n_z, 2, tok, 2 * D), BF),
            pltpu.VMEM((n_z, tok, D), BF),
            pltpu.VMEM((n_z, tok, D), BF),
            pltpu.VMEM((2 * tok, 2 * D), F32),
            pltpu.VMEM((n_ctx, heads, n_clu, D), BF),
            pltpu.VMEM((n_ctx, heads, n_clu, D), BF),
            pltpu.VMEM((n_clu * heads, D), F32),
            pltpu.VMEM((n_z * heads, D), F32),
            pltpu.VMEM((n_z * heads, D), F32),
            pltpu.VMEM((n_z, heads, D), F32),
            pltpu.VMEM((n_z, heads, D), F32),
            pltpu.VMEM((n_z * heads, D), BF),
            pltpu.VMEM((4, tok, D), BF),
            pltpu.VMEM((D + 16, tok), BF),
            dma((4,)),
            dma((4,)),
            dma((4,)),
            dma((heads,)),
            dma(()),
            dma((heads,)),
            dma(()),
            dma(()),
            dma((n_z,)),
            dma((4,)),
            dma(()),
            dma(()),
            dma(()),
            dma(()),
            dma((4,)),
            dma(()),
            dma(()),
            dma(()),
            dma(()),
            dma(()),
            dma(()),
        ],
        compiler_params=pltpu.CompilerParams(
            collective_id=0, has_side_effects=True, vmem_limit_bytes=60 * 1024 * 1024
        ),
        cost_estimate=pl.CostEstimate(
            flops=2 * 2 * 2 * D * tok * tok * n_clu * n_clu // 4,
            bytes_accessed=8 * tok * width,
            transcendentals=tok * tok * n_clu * n_clu // 4,
        ),
    )(queries, keys, values, clusters.T, centroids)
    fresh = jnp.transpose(fresh.reshape(2, n_ctx, n_z, heads, D), (2, 0, 1, 3, 4)).astype(F32)
    return attended, fresh.reshape(n_clu * n_ctx, heads, D)


def solution(mesh):
    placed = (
        P(("ctx", "clu"), None),
        P(("ctx", "clu"), None),
        P(("ctx", "clu"), None),
        P(("ctx", "clu"), None),
        P("clu", None, None),
    )
    return jax.shard_map(
        functools.partial(local, mesh.shape["ctx"], mesh.shape["clu"]),
        mesh=mesh,
        in_specs=placed,
        out_specs=(P(("ctx", "clu"), None), P()),
        check_vma=False,
    )
```
